128 devices in a mesh: cand: 2 (over core), dp: 64 (over x, y, z).
Axes of the slice: x: 4, y: 4, z: 4, core: 2. Of those that a mesh axis runs over, the one named last changes fastest.
Arguments:
- token_ids: int32 [64, 6, 64], P('dp', 'cand'), may hold values from 0 to 50303
- token_mask: int32 [64, 6, 32], P('dp', 'cand'), may hold values 0 or 1
- resp_lengths: int32 [64, 6], P('dp', 'cand'), may hold values from 1 to 32, as said below
- cand_counts: int32 [64], P('dp'), may hold values from 2 to 5
- cand_rank: int32 [64, 6], P('dp', 'cand'), may hold values from 0 to 5, each once within a row
- rewards: float32 [64, 6], P('dp', 'cand')
- embed_table: float32 [50304, 1024], P(None, 'dp'), may hold values from -0.6 to 0.6
- embed_first: float32 [50304, 1024], P(None, 'dp'), may hold values from -6.137985e-05 to 6.137985e-05
- embed_second: float32 [50304, 1024], P(None, 'dp'), may hold values from 8.648958e-12 to 3.4595833e-11
- head_table: float32 [50304, 1024], P('dp')
- head_first: float32 [50304, 1024], P('dp'), may hold values from -6.137985e-05 to 6.137985e-05
- head_second: float32 [50304, 1024], P('dp'), may hold values from 8.648958e-12 to 3.4595833e-11
- qkv_weight: float32 [1024, 3072], P(('cand', 'dp')), may hold values from -0.1875 to 0.1875
- qkv_first: float32 [1024, 3072], P(('cand', 'dp')), may hold values from -6.137985e-05 to 6.137985e-05
- qkv_second: float32 [1024, 3072], P(('cand', 'dp')), may hold values from 8.648958e-12 to 3.4595833e-11
- proj_weight: float32 [1024, 1024], P(('cand', 'dp')), may hold values from -0.5 to 0.5
- proj_first: float32 [1024, 1024], P(('cand', 'dp')), may hold values from -6.137985e-05 to 6.137985e-05
- proj_second: float32 [1024, 1024], P(('cand', 'dp')), may hold values from 8.648958e-12 to 3.4595833e-11
- up_weight: float32 [1024, 4096], P(('cand', 'dp')), may hold values from -0.1875 to 0.1875
- up_first: float32 [1024, 4096], P(('cand', 'dp')), may hold values from -6.137985e-05 to 6.137985e-05
- up_second: float32 [1024, 4096], P(('cand', 'dp')), may hold values from 8.648958e-12 to 3.4595833e-11
- down_weight: float32 [4096, 1024], P(('cand', 'dp')), may hold values from -0.09375 to 0.09375
- down_first: float32 [4096, 1024], P(('cand', 'dp')), may hold values from -6.137985e-05 to 6.137985e-05
- down_second: float32 [4096, 1024], P(('cand', 'dp')), may hold values from 8.648958e-12 to 3.4595833e-11
- vector_params: float32 [15360], replicated
- vector_first: float32 [15360], P(('cand', 'dp')), may hold values from -0.0006137985 to 0.0006137985
- vector_second: float32 [15360], P(('cand', 'dp')), may hold values from 8.648958e-10 to 3.4595833e-09
Outputs:
- loss_parts: float32 [3], replicated
- grad_norm: float32 [], replicated
- score_grads: float32 [64, 6], P('dp', 'cand')
- embed_first_new: float32 [50304, 1024], P(None, 'dp')
- embed_second_new: float32 [50304, 1024], P(None, 'dp')
- embed_table_new: float32 [50304, 1024], P(None, 'dp')
- head_first_new: float32 [50304, 1024], P('dp')
- head_second_new: float32 [50304, 1024], P('dp')
- head_table_new: float32 [50304, 1024], P('dp')
- qkv_first_new: float32 [1024, 3072], P(('cand', 'dp'))
- qkv_second_new: float32 [1024, 3072], P(('cand', 'dp'))
- qkv_weight_new: float32 [1024, 3072], P(('cand', 'dp'))
- proj_first_new: float32 [1024, 1024], P(('cand', 'dp'))
- proj_second_new: float32 [1024, 1024], P(('cand', 'dp'))
- proj_weight_new: float32 [1024, 1024], P(('cand', 'dp'))
- up_first_new: float32 [1024, 4096], P(('cand', 'dp'))
- up_second_new: float32 [1024, 4096], P(('cand', 'dp'))
- up_weight_new: float32 [1024, 4096], P(('cand', 'dp'))
- down_first_new: float32 [4096, 1024], P(('cand', 'dp'))
- down_second_new: float32 [4096, 1024], P(('cand', 'dp'))
- down_weight_new: float32 [4096, 1024], P(('cand', 'dp'))
- vector_first_new: float32 [15360], P(('cand', 'dp'))
- vector_second_new: float32 [15360], P(('cand', 'dp'))
The draws below stay inside these ranges and needn't reach their ends.
Inputs may be any that keep to these rules, and one draw needn't show every extreme that they name: `resp_lengths`: response lengths rise in spread with the prompt's index; 32 is reached in every draw. cand_rank orders the slots of a prompt; slots of rank below the prompt's count are its candidates.
All inputs are finite; a program needn't handle non-finite values. No bound on the sum of `token_mask` on one device may be relied on, other than what follows from the above.
Results may differ from the reference program's by a relative error of at most 0.03.
Values may be sent and summed in bfloat16 or wider, within the bound.
No kernel may reach another device: no remote copies, remote signals or barrier semaphores. Data moves between devices by JAX's collectives and lax.ppermute only.
A program may use at most 320 MiB of HBM per device.

```python
import math
import jax
import jax.numpy as jnp
from jax import lax

D = 1024
HEADS = 16
HEAD_DIM = 64
ROT = 16
FF = 4096
V = 50304
SEQ = 64
STEP = 10
RESP = 32
CANDS = 6
PROMPTS = 64
VEC = 15360
NPARAMS = 115620864


def draw_resp_lengths(key, part):
    key_one, key_two = jax.random.split(jax.random.fold_in(key, 11))
    first = jax.random.randint(key_one, (PROMPTS, CANDS), 1, RESP + 1)
    second = jax.random.randint(key_two, (PROMPTS, CANDS), 1, RESP + 1)
    shorter = jnp.minimum(first, second)
    rising = PROMPTS + 2 * jnp.arange(PROMPTS, dtype=jnp.int32)[:, None]
    scaled = 1 + (shorter - 1) * rising // (3 * PROMPTS - 2)
    return scaled.at[PROMPTS - 1, 0].set(RESP).astype(jnp.int32)


def draw_rewards(key, part):
    key = jax.random.fold_in(key, 13)
    index = jnp.arange(PROMPTS, dtype=jnp.float32)[:, None] / PROMPTS
    base = jax.random.normal(key, (PROMPTS, CANDS), jnp.float32)
    rising = 1.0 + 2.0 * index
    return base * rising


def draw_head_table(key, part):
    key = jax.random.fold_in(key, 17)
    index = jnp.arange(V, dtype=jnp.float32)[:, None] / V
    base = jax.random.normal(key, (V, D), jnp.float32)
    rising = 1.0 + 2.0 * index
    return base * rising * D ** (-0.5)


def draw_vector_params(key, part):
    key_one, key_two, key_three = jax.random.split(jax.random.fold_in(key, 7), 3)
    ramp = 0.5 + 1.5 * jnp.arange(D, dtype=jnp.float32) / D
    gains = ramp[None, :] * jax.random.uniform(key_one, (3, D), jnp.float32, 0.8, 1.2)
    shifts = 0.3 * jax.random.normal(key_two, (3, D), jnp.float32)
    blocks = jnp.stack([gains, shifts], axis=1).reshape(6 * D)
    others = 0.1 * jax.random.normal(key_three, (5 * D + FF,), jnp.float32)
    return jnp.concatenate([blocks, others])


def place_ends(values, rng, least, largest):
    dims = values.shape
    spot = [jax.random.randint(jax.random.fold_in(rng, axis), (), 0, dims[axis]) for axis in range(len(dims))]
    values = values.at[tuple(spot)].set(least)
    longest = dims.index(max(dims))
    spot[longest] = (spot[longest] + 1) % dims[longest]
    return values.at[tuple(spot)].set(largest)


def level_of(stream_key, extent, shards, smallest, high):
    factor_of, own = 1.0, jax.random.fold_in(stream_key, 6)
    for axis_at, blocks in shards:
        steps = jnp.exp(jax.random.uniform(jax.random.fold_in(own, axis_at), (blocks,), jnp.float32, smallest / len(shards), high / len(shards)))
        factor_of = factor_of * jnp.repeat(steps, extent[axis_at] // blocks).reshape([-1 if axis == axis_at else 1 for axis in range(len(extent))])
    return factor_of


def normal_values(rng, dims, deviation, reach, cuts=(), held_as=jnp.bfloat16):
    entries = deviation * jax.random.normal(rng, dims, jnp.float32)
    if cuts:
        entries = entries * level_of(rng, dims, cuts, -0.22, 0.18)
    return jnp.clip(entries, -reach, reach).astype(held_as)


def setup_inputs(seed: int = 0) -> dict:
    splits = jax.random.split(jax.random.key(seed), 28)
    return {
        "token_ids": place_ends(jax.random.randint(splits[0], (PROMPTS, CANDS, SEQ), 0, V), jax.random.fold_in(splits[0], 1), 0, V - 1).astype(jnp.int32),
        "token_mask": place_ends((jax.random.randint(splits[1], (PROMPTS, CANDS, RESP), 0, 8) < 7).astype(jnp.int32), jax.random.fold_in(splits[1], 1), 0, 1),
        "resp_lengths": draw_resp_lengths(jax.random.fold_in(splits[27], 71), 0),
        "cand_counts": place_ends(jax.random.randint(splits[3], (PROMPTS,), 2, CANDS), jax.random.fold_in(splits[3], 1), 2, CANDS - 1).astype(jnp.int32),
        "cand_rank": jax.vmap(lambda own: jax.random.permutation(own, CANDS))(jax.random.split(splits[4], PROMPTS)).reshape((PROMPTS, CANDS)).astype(jnp.int32),
        "rewards": draw_rewards(jax.random.fold_in(splits[27], 71), 0),
        "embed_table": normal_values(splits[6], (V, D), 0.1, 0.6, ((1, 64),), jnp.float32),
        "embed_first": normal_values(splits[7], (V, D), (0.11 / NPARAMS ** 0.5), 6.137984746601433e-05, ((1, 64),), jnp.float32),
        "embed_second": jnp.clip(jnp.exp(math.log(3.45958331426921e-11) - 1.3862944 * jax.random.uniform(splits[8], (V, D), jnp.float32) ** level_of(splits[8], (V, D), ((1, 64),), -0.2, 0.2)), 8.648958285673025e-12, 3.45958331426921e-11),
        "head_table": draw_head_table(jax.random.fold_in(splits[27], 71), 0),
        "head_first": normal_values(splits[10], (V, D), (0.11 / NPARAMS ** 0.5), 6.137984746601433e-05, ((0, 64),), jnp.float32),
        "head_second": jnp.clip(jnp.exp(math.log(3.45958331426921e-11) - 1.3862944 * jax.random.uniform(splits[11], (V, D), jnp.float32) ** level_of(splits[11], (V, D), ((0, 64),), -0.2, 0.2)), 8.648958285673025e-12, 3.45958331426921e-11),
        "qkv_weight": normal_values(splits[12], (D, 3 * D), D ** -0.5, 0.1875, ((0, 128),), jnp.float32),
        "qkv_first": normal_values(splits[13], (D, 3 * D), (0.11 / NPARAMS ** 0.5), 6.137984746601433e-05, ((0, 128),), jnp.float32),
        "qkv_second": jnp.clip(jnp.exp(math.log(3.45958331426921e-11) - 1.3862944 * jax.random.uniform(splits[14], (D, 3 * D), jnp.float32) ** level_of(splits[14], (D, 3 * D), ((0, 128),), -0.2, 0.2)), 8.648958285673025e-12, 3.45958331426921e-11),
        "proj_weight": normal_values(splits[15], (D, D), (D // 8) ** -0.5, 0.5, ((0, 128),), jnp.float32),
        "proj_first": normal_values(splits[16], (D, D), (0.11 / NPARAMS ** 0.5), 6.137984746601433e-05, ((0, 128),), jnp.float32),
        "proj_second": jnp.clip(jnp.exp(math.log(3.45958331426921e-11) - 1.3862944 * jax.random.uniform(splits[17], (D, D), jnp.float32) ** level_of(splits[17], (D, D), ((0, 128),), -0.2, 0.2)), 8.648958285673025e-12, 3.45958331426921e-11),
        "up_weight": normal_values(splits[18], (D, FF), D ** -0.5, 0.1875, ((0, 128),), jnp.float32),
        "up_first": normal_values(splits[19], (D, FF), (0.11 / NPARAMS ** 0.5), 6.137984746601433e-05, ((0, 128),), jnp.float32),
        "up_second": jnp.clip(jnp.exp(math.log(3.45958331426921e-11) - 1.3862944 * jax.random.uniform(splits[20], (D, FF), jnp.float32) ** level_of(splits[20], (D, FF), ((0, 128),), -0.2, 0.2)), 8.648958285673025e-12, 3.45958331426921e-11),
        "down_weight": normal_values(splits[21], (FF, D), FF ** -0.5, 0.09375, ((0, 128),), jnp.float32),
        "down_first": normal_values(splits[22], (FF, D), (0.11 / NPARAMS ** 0.5), 6.137984746601433e-05, ((0, 128),), jnp.float32),
        "down_second": jnp.clip(jnp.exp(math.log(3.45958331426921e-11) - 1.3862944 * jax.random.uniform(splits[23], (FF, D), jnp.float32) ** level_of(splits[23], (FF, D), ((0, 128),), -0.2, 0.2)), 8.648958285673025e-12, 3.45958331426921e-11),
        "vector_params": draw_vector_params(jax.random.fold_in(splits[27], 71), 0),
        "vector_first": normal_values(splits[25], (VEC,), (1.1 / NPARAMS ** 0.5), 0.0006137985, ((0, 128),), jnp.float32),
        "vector_second": jnp.clip(jnp.exp(math.log(3.4595832865136344e-09) - 1.3862944 * jax.random.uniform(splits[26], (VEC,), jnp.float32) ** level_of(splits[26], (VEC,), ((0, 128),), -0.2, 0.2)), 8.648958216284086e-10, 3.4595832865136344e-09),
    }


HIGH = lax.Precision.HIGHEST
NORM_EPS = 1e-05
CLIP_NORM = 1.0
LEARN_RATE = 0.05
BETA_ONE = 0.9
BETA_TWO = 0.999
ADAM_EPS = 1e-08
DECAY = 0.1

@jax.custom_vjp
def low(v):
    return lax.optimization_barrier(v.astype(jnp.bfloat16)).astype(jnp.float32)

@jax.custom_vjp
def low_back(v):
    return v

def low_keep(v):
    return (low(v), None)

def low_pass(kept, grad):
    return (grad,)

def back_keep(v):
    return (v, None)

def back_low(kept, grad):
    return (low(grad),)
low.defvjp(low_keep, low_pass)
low_back.defvjp(back_keep, back_low)

def matmul(left, right):
    return jnp.dot(left, right, precision=HIGH)

def layer_norm(inputs, gain, bias):
    mean = lax.optimization_barrier(jnp.mean(inputs, -1, keepdims=True))
    centred = inputs - mean
    variance = lax.optimization_barrier(jnp.mean(centred * centred, -1, keepdims=True))
    return centred * lax.rsqrt(variance + NORM_EPS) * gain + bias

def rotary(inputs, sign):
    seqlen = inputs.shape[-3]
    half = ROT // 2
    freq = 10000.0 ** (-jnp.arange(half).astype(jnp.float32) * (2.0 / ROT))
    angle = jnp.arange(seqlen).astype(jnp.float32)[:, None] * freq[None, :]
    cosine = jnp.cos(angle)[:, None, :]
    sine = sign * jnp.sin(angle)[:, None, :]
    first = inputs[..., :half]
    second = inputs[..., half:ROT]
    return jnp.concatenate([first * cosine - second * sine, second * cosine + first * sine, inputs[..., ROT:]], axis=-1)

def split_params(vector):
    spans = [D, D, D, D, D, D, 3 * D, D, FF, D]
    pieces = []
    begin = 0
    for span_len in spans:
        pieces.append(vector[begin:begin + span_len])
        begin = begin + span_len
    return pieces

def prompt_logp(weights, ids_prompt):
    embed, head, qkv_w, proj_w, up_w, down_w, vector = weights
    gain_one, bias_one, gain_two, bias_two, gain_fin, bias_fin, qkv_bias, proj_bias, up_bias, down_bias = split_params(vector)
    cands = ids_prompt.shape[0]
    inputs = embed[ids_prompt]
    attn_in = low(layer_norm(inputs, gain_one, bias_one))
    mlp_in = low(layer_norm(inputs, gain_two, bias_two))
    qkv = low_back(matmul(attn_in, qkv_w) + qkv_bias)
    query = low(rotary(qkv[..., :D].reshape(cands, SEQ, HEADS, HEAD_DIM), 1.0))
    keys = low(rotary(qkv[..., D:2 * D].reshape(cands, SEQ, HEADS, HEAD_DIM), 1.0))
    values = low(qkv[..., 2 * D:].reshape(cands, SEQ, HEADS, HEAD_DIM))
    scores = low_back(jnp.einsum('cqhd,ckhd->chqk', query, keys, precision=HIGH) * HEAD_DIM ** (-0.5))
    causal = jnp.arange(SEQ)[:, None] >= jnp.arange(SEQ)[None, :]
    probs = low(jax.nn.softmax(jnp.where(causal, scores, -1e+30), axis=-1))
    mixed = low(low_back(jnp.einsum('chqk,ckhd->cqhd', probs, values, precision=HIGH))).reshape(cands, SEQ, D)
    attn = low_back(matmul(mixed, proj_w) + proj_bias)
    up_val = low_back(matmul(mlp_in, up_w) + up_bias)
    act = low(jax.nn.gelu(up_val, approximate=False))
    mlp = low_back(matmul(act, down_w) + down_bias)
    hidden = inputs + attn + mlp
    rows = low(layer_norm(hidden[:, SEQ - RESP - 1:SEQ - 1], gain_fin, bias_fin))
    logits = low_back(matmul(rows, head.T))
    target = jnp.take_along_axis(logits, ids_prompt[:, SEQ - RESP:, None], axis=-1)[..., 0]
    return target - jax.nn.logsumexp(logits, axis=-1)

def pro_single(scores, weight, ranks, count):
    valid = ranks < count
    head = ranks < count - 1
    peak = jnp.max(jnp.where(valid, scores, -1e+30))
    expo = jnp.where(valid, jnp.exp(scores - peak), 0.0)
    later = ranks[None, :] >= ranks[:, None]
    suffix = lax.optimization_barrier(jnp.sum(jnp.where(later, expo[None, :], 0.0), -1))
    return jnp.sum(jnp.where(head, -weight * (scores - peak - jnp.log(jnp.where(head, suffix, 1.0))), 0.0))

def moments(first, second, grad, factor):
    clipped = grad * factor
    first_new = BETA_ONE * first + (1.0 - BETA_ONE) * clipped
    second_new = BETA_TWO * second + (1.0 - BETA_TWO) * clipped * clipped
    return (first_new, second_new)

def adam_update(weight, first, second, grad, factor):
    first_new, second_new = moments(first, second, grad, factor)
    first_hat = first_new / (1.0 - BETA_ONE ** STEP)
    second_hat = second_new / (1.0 - BETA_TWO ** STEP)
    weight_new = weight - LEARN_RATE * (first_hat / (jnp.sqrt(second_hat) + ADAM_EPS) + DECAY * weight)
    return (first_new, second_new, weight_new)

def reference(token_ids, token_mask, resp_lengths, cand_counts, cand_rank, rewards, embed_table, embed_first, embed_second, head_table, head_first, head_second, qkv_weight, qkv_first, qkv_second, proj_weight, proj_first, proj_second, up_weight, up_first, up_second, down_weight, down_first, down_second, vector_params, vector_first, vector_second):
    masters = (embed_table, head_table, qkv_weight, proj_weight, up_weight, down_weight, vector_params)

    def forward(params):
        rounded = tuple((low(w) for w in params[:6])) + (params[6],)
        step_fn = jax.checkpoint(lambda ids_prompt: prompt_logp(rounded, ids_prompt))
        return lax.map(step_fn, token_ids)
    logp, pullback = jax.vjp(forward, masters)
    live = ((jnp.arange(RESP)[None, None, :] < resp_lengths[:, :, None]) & (token_mask == 1)).astype(jnp.float32)
    count_tok = lax.optimization_barrier(jnp.sum(live, -1))
    valid = (cand_rank < cand_counts[:, None]).astype(jnp.float32)
    top = (cand_rank == 0).astype(jnp.float32)
    total = jnp.sum(valid)
    mean = jnp.sum(rewards * valid) / total
    variance = jnp.sum(rewards * rewards * valid) / total - mean * mean
    weight = jax.nn.softplus((rewards - mean) * lax.rsqrt(variance + NORM_EPS))
    sft_count = jnp.sum(live * top[..., None])

    def pro_of(scores):
        return jnp.sum(jax.vmap(pro_single)(scores, weight, cand_rank, cand_counts))

    def loss_of(logp_all):
        scores = lax.optimization_barrier(jnp.sum(logp_all * live, -1)) / jnp.maximum(count_tok, 1.0)
        sft_sum = -jnp.sum(logp_all * live * top[..., None])
        return pro_of(scores) + PROMPTS * sft_sum / jnp.maximum(sft_count, 1.0)
    grads = pullback(jax.grad(loss_of)(logp))[0]
    scores = lax.optimization_barrier(jnp.sum(logp * live, -1)) / jnp.maximum(count_tok, 1.0)
    pro_value, score_grads = jax.value_and_grad(pro_of)(scores)
    sft_sum = -jnp.sum(logp * live * top[..., None])
    loss_parts = jnp.stack([pro_value, sft_sum, sft_count])
    grad_norm = jnp.sqrt(sum((jnp.sum(g * g) for g in grads)))
    factor = jnp.minimum(1.0, CLIP_NORM / (grad_norm + 1e-06))
    firsts = (embed_first, head_first, qkv_first, proj_first, up_first, down_first)
    seconds = (embed_second, head_second, qkv_second, proj_second, up_second, down_second)
    new_all = [adam_update(masters[i], firsts[i], seconds[i], grads[i], factor) for i in range(6)]
    emb_new, head_new, qkv_new, proj_new, up_new, down_new = new_all
    vec_first, vec_second = moments(vector_first, vector_second, grads[6], factor)
    return (loss_parts, grad_norm, score_grads, emb_new[0], emb_new[1], emb_new[2], head_new[0], head_new[1], head_new[2], qkv_new[0], qkv_new[1], qkv_new[2], proj_new[0], proj_new[1], proj_new[2], up_new[0], up_new[1], up_new[2], down_new[0], down_new[1], down_new[2], vec_first, vec_second)
```

```python
import jax
import jax.numpy as jnp
from jax import lax
from jax.sharding import Mesh
from jax.sharding import PartitionSpec as P

D = 1024
HEADS = 16
HEAD_DIM = 64
ROT = 16
FF = 4096
SEQ = 64
STEP = 10
RESP = 32


NORM_EPS = 1e-05
CLIP_NORM = 1.0
LEARN_RATE = 0.05
BETA_ONE = 0.9
BETA_TWO = 0.999
ADAM_EPS = 1e-08
DECAY = 0.1


RING = 4
VOCAB_PAD = 896
AXES = ("x", "y", "z")


def shift(value, axis, step):
    return lax.ppermute(value, axis, [(i, (i + step) % RING) for i in range(RING)])


def swap(value):
    return lax.ppermute(value, "cand", [(0, 1), (1, 0)])


def near_gather(value, axis):
    return jnp.stack([value, shift(value, axis, -1), shift(value, axis, 2), shift(value, axis, 1)])


def near_scatter(pieces, axis):
    return [pieces[0], shift(pieces[1], axis, 1), shift(pieces[2], axis, 2), shift(pieces[3], axis, -1)]


def total(value, axis):
    near = shift(value, axis, 1) + shift(value, axis, -1)
    return (value + shift(value, axis, 2)) + near


def total_all(value):
    value = value + swap(value)
    for axis in AXES:
        value = total(value, axis)
    return value


def halves(value):
    mid = value.shape[-1] // 2
    return (value[..., :mid], value[..., mid:])


def ring_gather(value, axis):
    before = shift(value, axis, 1)
    after = shift(value, axis, -1)
    far = jnp.concatenate(
        [shift(halves(before)[0], axis, 1), shift(halves(after)[1], axis, -1)], axis=-1
    )
    return [value, after, far, before]


def add_low(first, second):
    return (first.astype(jnp.float32) + second.astype(jnp.float32)).astype(first.dtype)


def ring_scatter(chunks, axis):
    own, after, far, before = chunks
    far_a, far_b = halves(far)
    after_a, after_b = halves(after)
    before_a, before_b = halves(before)
    got_a = shift(far_a, axis, -1)
    got_b = shift(far_b, axis, 1)
    from_after_b = shift(before_b, axis, -1)
    from_before_a = shift(after_a, axis, 1)
    from_after_a = shift(add_low(before_a, got_a), axis, -1)
    from_before_b = shift(add_low(after_b, got_b), axis, 1)
    from_after = jnp.concatenate([from_after_a, from_after_b], axis=-1).astype(jnp.float32)
    from_before = jnp.concatenate([from_before_a, from_before_b], axis=-1).astype(jnp.float32)
    return own.astype(jnp.float32) + (from_after + from_before)


def rolled_chunks(value, axis, dim):
    me = lax.axis_index(axis)
    return [
        lax.dynamic_index_in_dim(value, (me + k) % RING, dim, keepdims=False) for k in range(RING)
    ]


def owner_sum(grad, order):
    rows = grad.shape[0] // 128
    parts = grad.reshape(2, 64 * rows, grad.shape[1])
    core = lax.axis_index("cand")
    sent = swap(lax.dynamic_index_in_dim(parts, 1 - core, 0, keepdims=False))
    kept = lax.dynamic_index_in_dim(parts, core, 0, keepdims=False)
    value = add_low(kept, sent).reshape(RING, RING, RING, rows, -1)
    left = list(AXES)
    for axis in order:
        dim = left.index(axis)
        value = ring_scatter(rolled_chunks(value, axis, dim), axis)
        left.remove(axis)
        if left:
            value = value.astype(jnp.bfloat16)
    return value


def owner_sum_small(vector):
    parts = vector.reshape(2, RING, RING, RING, -1)
    core = lax.axis_index("cand")
    sent = swap(lax.dynamic_index_in_dim(parts, 1 - core, 0, keepdims=False))
    value = lax.dynamic_index_in_dim(parts, core, 0, keepdims=False) + sent
    for axis in AXES:
        got = near_scatter(rolled_chunks(value, axis, 0), axis)
        value = (got[0] + got[2]) + (got[1] + got[3])
    return value


def matmul(left, right):
    return jnp.dot(left, right, preferred_element_type=jnp.float32)


def matmul_tn(left, right):
    return lax.dot_general(
        left, right, (((0,), (0,)), ((), ())), preferred_element_type=jnp.float32
    )


def matmul_nt(left, right):
    return lax.dot_general(
        left, right, (((1,), (1,)), ((), ())), preferred_element_type=jnp.float32
    )


def layer_norm(inputs, gain, bias):
    mean = jnp.mean(inputs, -1, keepdims=True)
    centred = inputs - mean
    variance = jnp.mean(centred * centred, -1, keepdims=True)
    return centred * lax.rsqrt(variance + NORM_EPS) * gain + bias


def norm_back(inputs, gain, bias, grad):
    outputs, pullback = jax.vjp(layer_norm, inputs, gain, bias)
    return pullback(grad)


def split_params(vector):
    spans = [D, D, D, D, D, D, 3 * D, D, FF, D]
    pieces = []
    begin = 0
    for span_len in spans:
        pieces.append(vector[begin : begin + span_len])
        begin = begin + span_len
    return pieces


def gelu_exact(values):
    return jax.nn.gelu(values, approximate=False)


def rotary(inputs, places, sign):
    half = ROT // 2
    freq = 10000.0 ** (-jnp.arange(half).astype(jnp.float32) * (2.0 / ROT))
    angle = places.astype(jnp.float32)[:, None] * freq[None, :]
    cosine = jnp.cos(angle)[:, None, :]
    sine = sign * jnp.sin(angle)[:, None, :]
    first = inputs[..., :half]
    second = inputs[..., half:ROT]
    return jnp.concatenate(
        [first * cosine - second * sine, second * cosine + first * sine, inputs[..., ROT:]], axis=-1
    )


def key_places():
    return (jnp.arange(SEQ) + (SEQ - RESP - 1)) % SEQ


def attention_probs(query, keys):
    scores = jnp.einsum(
        "cqhd,ckhd->chqk", query, keys, preferred_element_type=jnp.float32
    ) * HEAD_DIM ** (-0.5)
    places = key_places()
    causal = places[:RESP, None] >= places[None, :]
    return jax.nn.softmax(jnp.where(causal, scores, -1e30), axis=-1)


def joined(rows, slots):
    cut = rows.reshape(2, slots, RESP, *rows.shape[1:])
    return jnp.concatenate([cut[0], cut[1]], axis=1)


def parted(rows):
    cut = jnp.stack([rows[:, :RESP], rows[:, RESP:]])
    return cut.reshape(-1, *rows.shape[2:])


def layer_forward(inputs, mats, pieces):
    query_w, kv_w, proj_w, up_w, down_w = mats
    live = inputs.shape[0] // 2
    slots = live // RESP
    first = inputs[:live]
    attn_in = layer_norm(inputs, pieces[0], pieces[1]).astype(jnp.bfloat16)
    mlp_in = layer_norm(first, pieces[2], pieces[3]).astype(jnp.bfloat16)
    query = matmul(attn_in[:live], query_w) + pieces[6][:D]
    both = matmul(attn_in, kv_w) + pieces[6][D:]
    query = rotary(query.reshape(slots, RESP, HEADS, HEAD_DIM), key_places()[:RESP], 1.0)
    keys = joined(both[:, :D], slots).reshape(slots, SEQ, HEADS, HEAD_DIM)
    keys = rotary(keys, key_places(), 1.0)
    values = joined(both[:, D:], slots).reshape(slots, SEQ, HEADS, HEAD_DIM)
    query, keys, values = [part.astype(jnp.bfloat16) for part in (query, keys, values)]
    probs_low = attention_probs(query, keys).astype(jnp.bfloat16)
    mixed = jnp.einsum("chqk,ckhd->cqhd", probs_low, values, preferred_element_type=jnp.float32)
    mixed = mixed.astype(jnp.bfloat16).reshape(-1, D)
    up_val = matmul(mlp_in, up_w) + pieces[8]
    act = gelu_exact(up_val).astype(jnp.bfloat16)
    hidden = first + (matmul(mixed, proj_w) + pieces[7]) + (matmul(act, down_w) + pieces[9])
    return (hidden, (attn_in, mlp_in, query, keys, values, mixed, up_val, act))


def layer_backward(inputs, saved, mats, pieces, grad_hidden):
    query_w, kv_w, proj_w, up_w, down_w = mats
    attn_in, mlp_in, query, keys, values, mixed, up_val, act = saved
    live = inputs.shape[0] // 2
    slots = live // RESP
    first = inputs[:live]
    grad_low = grad_hidden.astype(jnp.bfloat16)
    grad_sum = jnp.sum(grad_low.astype(jnp.float32), 0)
    down_grad = matmul_tn(act, grad_low).astype(jnp.bfloat16)
    act_grad = matmul_nt(grad_low, down_w)
    gelu_out, gelu_pull = jax.vjp(gelu_exact, up_val)
    up_grad_low = gelu_pull(act_grad)[0].astype(jnp.bfloat16)
    up_w_grad = matmul_tn(mlp_in, up_grad_low).astype(jnp.bfloat16)
    mlp_in_grad = matmul_nt(up_grad_low, up_w)
    proj_grad = matmul_tn(mixed, grad_low).astype(jnp.bfloat16)
    mixed_grad = (
        matmul_nt(grad_low, proj_w).astype(jnp.bfloat16).reshape(slots, RESP, HEADS, HEAD_DIM)
    )
    probs = attention_probs(query, keys)
    probs_low = probs.astype(jnp.bfloat16)
    probs_grad = jnp.einsum(
        "cqhd,ckhd->chqk", mixed_grad, values, preferred_element_type=jnp.float32
    )
    value_grad = jnp.einsum(
        "chqk,cqhd->ckhd", probs_low, mixed_grad, preferred_element_type=jnp.float32
    )
    score_grad = probs * (probs_grad - jnp.sum(probs * probs_grad, -1, keepdims=True))
    score_grad = score_grad.astype(jnp.bfloat16)
    scale = HEAD_DIM ** (-0.5)
    query_grad = (
        jnp.einsum("chqk,ckhd->cqhd", score_grad, keys, preferred_element_type=jnp.float32) * scale
    )
    key_grad = (
        jnp.einsum("chqk,cqhd->ckhd", score_grad, query, preferred_element_type=jnp.float32) * scale
    )
    query_grad = rotary(query_grad, key_places()[:RESP], -1.0).reshape(live, D)
    key_grad = rotary(key_grad, key_places(), -1.0).reshape(slots, SEQ, D)
    value_grad = value_grad.reshape(slots, SEQ, D)
    query_grad = query_grad.astype(jnp.bfloat16)
    both_grad = jnp.concatenate([parted(key_grad), parted(value_grad)], axis=1).astype(jnp.bfloat16)
    qkv_w_grad = jnp.concatenate(
        [
            matmul_tn(attn_in[:live], query_grad).astype(jnp.bfloat16),
            matmul_tn(attn_in, both_grad).astype(jnp.bfloat16),
        ],
        axis=1,
    )
    attn_in_grad = matmul_nt(both_grad, kv_w)
    attn_in_grad = attn_in_grad + jnp.pad(matmul_nt(query_grad, query_w), ((0, live), (0, 0)))
    input_one, gain_one_grad, bias_one_grad = norm_back(inputs, pieces[0], pieces[1], attn_in_grad)
    input_two, gain_two_grad, bias_two_grad = norm_back(first, pieces[2], pieces[3], mlp_in_grad)
    input_grad = input_one + jnp.pad(grad_hidden + input_two, ((0, live), (0, 0)))
    vector_head = [gain_one_grad, bias_one_grad, gain_two_grad, bias_two_grad]
    vector_tail = [
        jnp.sum(query_grad.astype(jnp.float32), 0),
        jnp.sum(both_grad.astype(jnp.float32), 0),
        grad_sum,
        jnp.sum(up_grad_low.astype(jnp.float32), 0),
        grad_sum,
    ]
    return (input_grad, (qkv_w_grad, proj_grad, up_w_grad, down_grad), vector_head, vector_tail)


def pro_single(scores, weight, ranks, count):
    valid = ranks < count
    head = ranks < count - 1
    peak = jnp.max(jnp.where(valid, scores, -1e30))
    expo = jnp.where(valid, jnp.exp(scores - peak), 0.0)
    later = ranks[None, :] >= ranks[:, None]
    suffix = jnp.sum(jnp.where(later, expo[None, :], 0.0), -1)
    return jnp.sum(
        jnp.where(head, -weight * (scores - peak - jnp.log(jnp.where(head, suffix, 1.0))), 0.0)
    )


def moments(first, second, grad, factor):
    clipped = grad * factor
    first_new = BETA_ONE * first + (1.0 - BETA_ONE) * clipped
    second_new = BETA_TWO * second + (1.0 - BETA_TWO) * clipped * clipped
    return (first_new, second_new)


def adam_update(weight, first, second, grad, factor):
    first_new, second_new = moments(first, second, grad, factor)
    first_hat = first_new / (1.0 - BETA_ONE**STEP)
    second_hat = second_new / (1.0 - BETA_TWO**STEP)
    weight_new = weight - LEARN_RATE * (
        first_hat / (jnp.sqrt(second_hat) + ADAM_EPS) + DECAY * weight
    )
    return (first_new, second_new, weight_new)


def body(
    token_ids,
    token_mask,
    resp_lengths,
    cand_counts,
    cand_rank,
    rewards,
    embed_table,
    embed_first,
    embed_second,
    head_table,
    head_first,
    head_second,
    qkv_weight,
    qkv_first,
    qkv_second,
    proj_weight,
    proj_first,
    proj_second,
    up_weight,
    up_first,
    up_second,
    down_weight,
    down_first,
    down_second,
    vector_params,
    vector_first,
    vector_second,
):
    slots = token_ids.shape[1]
    rows_own = slots * RESP
    core = lax.axis_index("cand")
    here = [lax.axis_index(axis) for axis in AXES]
    vocab_local = head_table.shape[0]
    pieces = split_params(vector_params)

    packed = jnp.concatenate(
        [
            qkv_weight.astype(jnp.bfloat16),
            up_weight.astype(jnp.bfloat16),
            proj_weight.astype(jnp.bfloat16),
            down_weight.astype(jnp.bfloat16).reshape(4, 8, D).transpose(1, 0, 2).reshape(8, 4 * D),
        ],
        axis=1,
    )
    gathered = lax.all_gather(packed, ("cand", "x", "y", "z"), axis=0, tiled=True)
    mats = (
        gathered[:, :D],
        gathered[:, D : 3 * D],
        gathered[:, 7 * D : 8 * D],
        gathered[:, 3 * D : 7 * D],
        gathered[:, 8 * D :].reshape(128, 8, 4, D).transpose(0, 2, 1, 3).reshape(FF, D),
    )

    turned = jnp.concatenate(
        [token_ids[0, :, SEQ - RESP - 1 :], token_ids[0, :, : SEQ - RESP - 1]], axis=1
    )
    near_ids = near_gather(near_gather(near_gather(turned, "z"), "y"), "x")
    group_targets = near_ids[:, :, 0, :, 1 : RESP + 1].reshape(-1)
    all_ids = near_ids
    for dim in range(3):
        twice = jnp.concatenate([all_ids, all_ids], axis=dim)
        all_ids = lax.dynamic_slice_in_dim(twice, (RING - here[dim]) % RING, RING, axis=dim)
    flat_ids = all_ids.reshape(64, slots, 2, RESP).transpose(0, 2, 1, 3).reshape(-1)
    looked = jnp.take(embed_table.astype(jnp.bfloat16), flat_ids, axis=0)
    inputs = lax.all_to_all(looked, AXES, split_axis=0, concat_axis=1, tiled=True).astype(
        jnp.float32
    )

    head_low = jnp.pad(head_table.astype(jnp.bfloat16), ((0, VOCAB_PAD - vocab_local), (0, 0)))
    head_half = lax.dynamic_slice_in_dim(head_low, core * (VOCAB_PAD // 2), VOCAB_PAD // 2)
    mine = jnp.stack(ring_gather(head_half, "z")[1:])
    theirs = swap(mine)
    ordered = jnp.where(
        core == 0, jnp.stack([mine, theirs], axis=1), jnp.stack([theirs, mine], axis=1)
    )
    head_group = jnp.concatenate([head_low, ordered.reshape(-1, D)], axis=0)

    live = (
        (jnp.arange(RESP)[None, None, :] < resp_lengths[:, :, None]) & (token_mask == 1)
    ).astype(jnp.float32)
    valid = (cand_rank < cand_counts[:, None]).astype(jnp.float32)
    top_mask = (cand_rank == 0).astype(jnp.float32)
    stats = total_all(
        jnp.stack(
            [
                jnp.sum(valid),
                jnp.sum(rewards * valid),
                jnp.sum(rewards * rewards * valid),
                jnp.sum(live * top_mask[..., None]),
            ]
        )
    )
    mean = stats[1] / stats[0]
    variance = stats[2] / stats[0] - mean * mean

    def pair(value):
        other = swap(value)
        return jnp.where(
            core == 0, jnp.concatenate([value, other]), jnp.concatenate([other, value])
        )

    all_rank = pair(cand_rank.reshape(-1))
    weight = jax.nn.softplus((pair(rewards.reshape(-1)) - mean) * lax.rsqrt(variance + NORM_EPS))

    hidden, saved = layer_forward(inputs, mats, pieces)
    rows_low = layer_norm(hidden, pieces[4], pieces[5]).astype(jnp.bfloat16)

    half_one, half_two = halves(rows_low)
    half_one = jnp.stack(ring_gather(jnp.stack(ring_gather(half_one, "y")), "x"))
    half_two = jnp.stack(ring_gather(jnp.stack(ring_gather(half_two, "x")), "y"))
    group_rows = jnp.concatenate([half_one, half_two.swapaxes(0, 1)], axis=-1).reshape(-1, D)

    shard = group_targets // vocab_local
    place = (shard % RING - here[2]) % RING
    local = (shard // RING) == here[0] * RING + here[1]
    targets = jnp.where(local, place * VOCAB_PAD + group_targets % vocab_local, -1)
    column = jnp.arange(RING * VOCAB_PAD)[None, :]
    logits = jnp.where(column % VOCAB_PAD < vocab_local, matmul_nt(group_rows, head_group), -1e30)
    hits = column == targets[:, None]
    local_max = jnp.max(logits, -1)
    local_sum = jnp.sum(jnp.exp(logits - local_max[:, None]), -1)
    local_target = jnp.sum(jnp.where(hits, logits, 0.0), -1)

    held = jnp.stack([local_max, local_sum, local_target]).reshape(3, RING, RING, rows_own)
    for axis in ("x", "y"):
        got = jnp.stack(near_scatter([held[:, k] for k in range(RING)], axis))
        biggest = jnp.max(got[:, 0], 0)
        held = jnp.stack(
            [
                biggest,
                jnp.sum(got[:, 1] * jnp.exp(got[:, 0] - biggest), 0),
                jnp.sum(got[:, 2], 0),
            ]
        )
    row_lse = held[0] + jnp.log(held[1])
    own_logp = (held[2] - row_lse).reshape(1, slots, RESP)
    own_count = jnp.sum(live, -1)
    own_scores = jnp.sum(own_logp * live, -1) / jnp.maximum(own_count, 1.0)
    all_scores = pair(own_scores.reshape(-1))
    pro_value, pro_grad = jax.value_and_grad(pro_single)(
        all_scores, weight, all_rank, cand_counts[0]
    )
    my_grad = lax.dynamic_slice_in_dim(pro_grad, core * slots, slots).reshape(1, slots)
    sft_scale = 64 / jnp.maximum(stats[3], 1.0)
    row_grad = (
        my_grad[..., None] / jnp.maximum(own_count, 1.0)[..., None]
        - sft_scale * top_mask[..., None]
    ) * live
    back = jnp.stack([row_grad.reshape(-1), row_lse])
    back = near_gather(near_gather(back, "y"), "x")
    group_grad = back[:, :, 0].reshape(-1)
    group_lse = back[:, :, 1].reshape(-1)

    vocab_probs = jnp.exp(logits - group_lse[:, None])
    logit_grad = (group_grad[:, None] * (hits.astype(jnp.float32) - vocab_probs)).astype(
        jnp.bfloat16
    )
    rows_part = matmul(logit_grad, head_group).astype(jnp.bfloat16)
    rows_part = rows_part.reshape(RING, RING, rows_own, D)
    part_one, part_two = halves(rows_part)
    part_one = ring_scatter([part_one[k] for k in range(RING)], "x").astype(jnp.bfloat16)
    part_one = ring_scatter([part_one[k] for k in range(RING)], "y")
    part_two = ring_scatter([part_two[:, k] for k in range(RING)], "y").astype(jnp.bfloat16)
    part_two = ring_scatter([part_two[k] for k in range(RING)], "x")
    rows_grad = jnp.concatenate([part_one, part_two], axis=-1)

    grad_hidden, gain_fin_grad, bias_fin_grad = norm_back(hidden, pieces[4], pieces[5], rows_grad)
    input_grad, mat_grads, vector_head, vector_tail = layer_backward(
        inputs, saved, mats, pieces, grad_hidden
    )

    head_part = matmul_tn(logit_grad, group_rows).astype(jnp.bfloat16)
    head_part = head_part.reshape(RING, 2, VOCAB_PAD // 2, D)
    sent = swap(lax.dynamic_index_in_dim(head_part, 1 - core, 1, keepdims=False))
    kept = lax.dynamic_index_in_dim(head_part, core, 1, keepdims=False)
    head_part = add_low(kept, sent)
    head_own = ring_scatter([head_part[k] for k in range(RING)], "z")
    head_other = swap(head_own)
    head_grad = jnp.where(
        core == 0,
        jnp.concatenate([head_own, head_other]),
        jnp.concatenate([head_other, head_own]),
    )[:vocab_local]

    embed_rows = lax.all_to_all(input_grad, AXES, split_axis=1, concat_axis=0, tiled=True)
    embed_grad = jax.ops.segment_sum(embed_rows, flat_ids, num_segments=embed_table.shape[0])
    embed_grad = embed_grad + swap(embed_grad)

    vector_grad = jnp.concatenate(vector_head + [gain_fin_grad, bias_fin_grad] + vector_tail)
    shards = (
        owner_sum(mat_grads[0], ("z", "x", "y")),
        owner_sum(mat_grads[1], ("z", "x", "y")),
        owner_sum(mat_grads[2], ("y", "z", "x")),
        owner_sum(mat_grads[3], ("x", "y", "z")),
        owner_sum_small(vector_grad),
    )
    local_squares = sum((jnp.sum(piece * piece) for piece in shards))
    local_squares = (
        local_squares + (jnp.sum(embed_grad * embed_grad) + jnp.sum(head_grad * head_grad)) / 2
    )
    sft_local = -jnp.sum(own_logp * live * top_mask[..., None])
    sums = total_all(jnp.stack([local_squares, pro_value / 2, sft_local]))
    grad_norm = jnp.sqrt(sums[0])
    factor = jnp.minimum(1.0, CLIP_NORM / (grad_norm + 1e-06))
    embed_new = adam_update(embed_table, embed_first, embed_second, embed_grad, factor)
    head_new = adam_update(head_table, head_first, head_second, head_grad, factor)
    qkv_new = adam_update(qkv_weight, qkv_first, qkv_second, shards[0], factor)
    proj_new = adam_update(proj_weight, proj_first, proj_second, shards[1], factor)
    up_new = adam_update(up_weight, up_first, up_second, shards[2], factor)
    down_new = adam_update(down_weight, down_first, down_second, shards[3], factor)
    vector_first_new, vector_second_new = moments(vector_first, vector_second, shards[4], factor)
    loss_parts = jnp.stack([sums[1], sums[2], stats[3]])
    return (
        loss_parts,
        grad_norm,
        my_grad,
        embed_new[0],
        embed_new[1],
        embed_new[2],
        head_new[0],
        head_new[1],
        head_new[2],
        qkv_new[0],
        qkv_new[1],
        qkv_new[2],
        proj_new[0],
        proj_new[1],
        proj_new[2],
        up_new[0],
        up_new[1],
        up_new[2],
        down_new[0],
        down_new[1],
        down_new[2],
        vector_first_new,
        vector_second_new,
    )


def solution(mesh):
    fine = Mesh(mesh.devices.reshape(2, RING, RING, RING), ("cand", *AXES))
    in_specs = (
        P(AXES, "cand", None),
        P(AXES, "cand", None),
        P(AXES, "cand"),
        P(AXES),
        P(AXES, "cand"),
        P(AXES, "cand"),
        P(None, AXES),
        P(None, AXES),
        P(None, AXES),
        P(AXES, None),
        P(AXES, None),
        P(AXES, None),
        P(("cand", *AXES), None),
        P(("cand", *AXES), None),
        P(("cand", *AXES), None),
        P(("cand", *AXES), None),
        P(("cand", *AXES), None),
        P(("cand", *AXES), None),
        P(("cand", *AXES), None),
        P(("cand", *AXES), None),
        P(("cand", *AXES), None),
        P(("cand", *AXES), None),
        P(("cand", *AXES), None),
        P(("cand", *AXES), None),
        P(),
        P(("cand", *AXES)),
        P(("cand", *AXES)),
    )
    out_specs = (
        P(),
        P(),
        P(AXES, "cand"),
        P(None, AXES),
        P(None, AXES),
        P(None, AXES),
        P(AXES, None),
        P(AXES, None),
        P(AXES, None),
        P(("cand", *AXES), None),
        P(("cand", *AXES), None),
        P(("cand", *AXES), None),
        P(("cand", *AXES), None),
        P(("cand", *AXES), None),
        P(("cand", *AXES), None),
        P(("cand", *AXES), None),
        P(("cand", *AXES), None),
        P(("cand", *AXES), None),
        P(("cand", *AXES), None),
        P(("cand", *AXES), None),
        P(("cand", *AXES), None),
        P(("cand", *AXES)),
        P(("cand", *AXES)),
    )
    return jax.shard_map(body, mesh=fine, in_specs=in_specs, out_specs=out_specs, check_vma=False)
```

```python
import jax
import jax.numpy as jnp
from jax import lax
from jax.experimental import pallas as pl
from jax.experimental.pallas import tpu as pltpu
from jax.sharding import Mesh
from jax.sharding import PartitionSpec as P

D = 1024
HEADS = 16
HEAD_DIM = 64
ROT = 16
FF = 4096
SEQ = 64
STEP = 10
RESP = 32


NORM_EPS = 1e-05
CLIP_NORM = 1.0
LEARN_RATE = 0.05
BETA_ONE = 0.9
BETA_TWO = 0.999
ADAM_EPS = 1e-08
DECAY = 0.1


RING = 4
PAD_HALF = 448
AXES = ("x", "y", "z")


def swap(value):
    return lax.ppermute(value, "cand", [(0, 1), (1, 0)])


def exchange(pieces, axes):
    return lax.all_to_all(pieces, axes, split_axis=0, concat_axis=0, tiled=True)


def spread(value, axes):
    count = lax.axis_size(axes)
    return exchange(jnp.broadcast_to(value[None], (count, *value.shape)), axes)


def core_sum(left, right, low=jnp.bfloat16):
    core = lax.axis_index("cand")
    half = left.shape[1] // 2
    kept = lax.dynamic_slice_in_dim(left, core * half, half, axis=1)
    given = lax.dynamic_slice_in_dim(left, (1 - core) * half, half, axis=1)
    return (
        matmul_tn(kept, right) + swap(matmul_tn(given, right).astype(low)).astype(jnp.float32)
    ).astype(low)


WIDE = 256
LOOK_BLOCK = 1024
FOLD_BLOCK = 2048


def look_kernel(high_ref, low_ref, table_ref, out_ref, left):
    spans = table_ref.shape[1] // WIDE
    rest = table_ref.shape[1] - spans * WIDE

    @pl.when(pl.program_id(0) == 0)
    def _():
        def fill(i, carry):
            span = table_ref[:, pl.ds(pl.multiple_of(i * WIDE, WIDE), WIDE)]
            left[pl.ds(pl.multiple_of(i * 16, 16), 16), :] = span.astype(jnp.bfloat16)
            return carry

        lax.fori_loop(0, spans, fill, 0)
        if rest:
            last = table_ref[:, spans * WIDE :].astype(jnp.bfloat16)
            left[spans * 16 :, :] = jnp.concatenate(
                [last, jnp.zeros((16, WIDE - rest), jnp.bfloat16)], axis=1
            )

    block = out_ref.shape[1]
    one_hot = jnp.where(
        lax.broadcasted_iota(jnp.int32, (WIDE, block), 0) == low_ref[...], 1.0, 0.0
    ).astype(jnp.bfloat16)
    high = jnp.broadcast_to(high_ref[...], (16, block))
    total = jnp.zeros((16, block), jnp.float32)
    rows = left.shape[0] // 16
    CH = 16
    for begin in range(0, rows, CH):
        count = min(CH, rows - begin)
        part = jnp.dot(
            left[begin * 16 : (begin + count) * 16, :], one_hot, preferred_element_type=jnp.float32
        )
        for k in range(count):
            total = total + jnp.where(high == begin + k, part[k * 16 : (k + 1) * 16], 0.0)
    out_ref[...] = total.astype(out_ref.dtype)


def look_up(table, ids):
    count = ids.shape[0]
    spans = -(-table.shape[1] // WIDE)
    high = (ids // WIDE).reshape(1, count)
    low = (ids % WIDE).reshape(1, count)
    row = pl.BlockSpec((1, LOOK_BLOCK), lambda i: (0, i))
    return pl.pallas_call(
        look_kernel,
        grid=(count // LOOK_BLOCK,),
        in_specs=[row, row, pl.BlockSpec(table.shape, lambda i: (0, 0))],
        out_specs=pl.BlockSpec((16, LOOK_BLOCK), lambda i: (0, i)),
        out_shape=jax.ShapeDtypeStruct((16, count), jnp.float32),
        scratch_shapes=[pltpu.VMEM((spans * 16, WIDE), jnp.bfloat16)],
        compiler_params=pltpu.CompilerParams(vmem_limit_bytes=40 << 20),
        cost_estimate=pl.CostEstimate(flops=2 * spans * 16 * WIDE * count, bytes_accessed=table.size * 4, transcendentals=0),
        name="look_up",
    )(high, low, table)


def fold_kernel(high_ref, low_ref, grad_ref, out_ref, left, total):
    step = pl.program_id(0)
    block = grad_ref.shape[1]
    rows = left.shape[0] // 16
    grad = grad_ref[...]
    high = jnp.broadcast_to(high_ref[...], (16, block))

    def place(i, carry):
        for k in range(4):
            at = i * 4 + k
            left[pl.ds(pl.multiple_of(at * 16, 16), 16), :] = jnp.where(
                high == at, grad, 0.0
            ).astype(jnp.bfloat16)
        return carry

    lax.fori_loop(0, rows // 4, place, 0)
    for at in range(rows // 4 * 4, rows):
        left[at * 16 : at * 16 + 16, :] = jnp.where(high == at, grad, 0.0).astype(jnp.bfloat16)
    one_hot = jnp.where(
        lax.broadcasted_iota(jnp.int32, (WIDE, block), 0) == low_ref[...], 1.0, 0.0
    ).astype(jnp.bfloat16)
    part = lax.dot_general(
        left[...], one_hot, (((1,), (1,)), ((), ())), preferred_element_type=jnp.float32
    )

    @pl.when(step == 0)
    def _():
        total[...] = part

    @pl.when(step > 0)
    def _():
        total[...] += part

    @pl.when(step == pl.num_programs(0) - 1)
    def _():
        spans = out_ref.shape[1] // WIDE
        rest = out_ref.shape[1] - spans * WIDE

        def drain(i, carry):
            out_ref[:, pl.ds(pl.multiple_of(i * WIDE, WIDE), WIDE)] = total[
                pl.ds(pl.multiple_of(i * 16, 16), 16), :
            ]
            return carry

        lax.fori_loop(0, spans, drain, 0)
        if rest:
            out_ref[:, spans * WIDE :] = total[spans * 16 :, :rest]


def fold(grads, ids, size):
    count = ids.shape[0]
    spans = -(-size // WIDE)
    high = (ids // WIDE).reshape(1, count)
    low = (ids % WIDE).reshape(1, count)
    row = pl.BlockSpec((1, FOLD_BLOCK), lambda i: (0, i))
    return pl.pallas_call(
        fold_kernel,
        grid=(count // FOLD_BLOCK,),
        in_specs=[row, row, pl.BlockSpec((16, FOLD_BLOCK), lambda i: (0, i))],
        out_specs=pl.BlockSpec((16, size), lambda i: (0, 0)),
        out_shape=jax.ShapeDtypeStruct((16, size), jnp.float32),
        scratch_shapes=[
            pltpu.VMEM((spans * 16, FOLD_BLOCK), jnp.bfloat16),
            pltpu.VMEM((spans * 16, WIDE), jnp.float32),
        ],
        compiler_params=pltpu.CompilerParams(vmem_limit_bytes=40 << 20),
        cost_estimate=pl.CostEstimate(flops=2 * spans * 16 * WIDE * count, bytes_accessed=size * 64, transcendentals=0),
        name="fold",
    )(high, low, grads)


def matmul(left, right):
    return jnp.dot(left, right, preferred_element_type=jnp.float32)


def matmul_tn(left, right):
    return lax.dot_general(
        left, right, (((0,), (0,)), ((), ())), preferred_element_type=jnp.float32
    )


def matmul_nt(left, right):
    return lax.dot_general(
        left, right, (((1,), (1,)), ((), ())), preferred_element_type=jnp.float32
    )


def layer_norm(inputs, gain, bias):
    mean = jnp.mean(inputs, -1, keepdims=True)
    centred = inputs - mean
    variance = jnp.mean(centred * centred, -1, keepdims=True)
    return centred * lax.rsqrt(variance + NORM_EPS) * gain + bias


def norm_back(inputs, gain, bias, grad):
    outputs, pullback = jax.vjp(layer_norm, inputs, gain, bias)
    return pullback(grad)


def split_params(vector):
    spans = [D, D, D, D, D, D, 3 * D, D, FF, D]
    pieces = []
    begin = 0
    for span_len in spans:
        pieces.append(vector[begin : begin + span_len])
        begin = begin + span_len
    return pieces


def gelu_exact(values):
    return jax.nn.gelu(values, approximate=False)


def rotary(inputs, places, sign):
    half = ROT // 2
    freq = 10000.0 ** (-jnp.arange(half).astype(jnp.float32) * (2.0 / ROT))
    angle = places.astype(jnp.float32)[:, None] * freq[None, :]
    cosine = jnp.cos(angle)[:, None, :]
    sine = sign * jnp.sin(angle)[:, None, :]
    first = inputs[..., :half]
    second = inputs[..., half:ROT]
    return jnp.concatenate(
        [first * cosine - second * sine, second * cosine + first * sine, inputs[..., ROT:]], axis=-1
    )


def key_places():
    return (jnp.arange(SEQ) + (SEQ - RESP - 1)) % SEQ


def attention_probs(query, keys):
    scores = jnp.einsum(
        "cqhd,ckhd->chqk", query, keys, preferred_element_type=jnp.float32
    ) * HEAD_DIM ** (-0.5)
    places = key_places()
    causal = places[:RESP, None] >= places[None, :]
    return jax.nn.softmax(jnp.where(causal, scores, -1e30), axis=-1)


def joined(rows, slots):
    cut = rows.reshape(2, slots, RESP, *rows.shape[1:])
    return jnp.concatenate([cut[0], cut[1]], axis=1)


def parted(rows):
    cut = jnp.stack([rows[:, :RESP], rows[:, RESP:]])
    return cut.reshape(-1, *rows.shape[2:])


def layer_forward(inputs, mats, pieces):
    query_w, kv_w, proj_w, up_w, down_w = mats
    live = inputs.shape[0] // 2
    slots = live // RESP
    first = inputs[:live]
    attn_in = layer_norm(inputs, pieces[0], pieces[1]).astype(jnp.bfloat16)
    mlp_in = layer_norm(first, pieces[2], pieces[3]).astype(jnp.bfloat16)
    query = matmul(attn_in[:live], query_w) + pieces[6][:D]
    both = matmul(attn_in, kv_w) + pieces[6][D:]
    query = rotary(query.reshape(slots, RESP, HEADS, HEAD_DIM), key_places()[:RESP], 1.0)
    keys = joined(both[:, :D], slots).reshape(slots, SEQ, HEADS, HEAD_DIM)
    keys = rotary(keys, key_places(), 1.0)
    values = joined(both[:, D:], slots).reshape(slots, SEQ, HEADS, HEAD_DIM)
    query, keys, values = [part.astype(jnp.bfloat16) for part in (query, keys, values)]
    probs_low = attention_probs(query, keys).astype(jnp.bfloat16)
    mixed = jnp.einsum("chqk,ckhd->cqhd", probs_low, values, preferred_element_type=jnp.float32)
    mixed = mixed.astype(jnp.bfloat16).reshape(-1, D)
    up_val = matmul(mlp_in, up_w) + pieces[8]
    act = gelu_exact(up_val).astype(jnp.bfloat16)
    mlp = sum(matmul(act[:, k * D : (k + 1) * D], part) for k, part in enumerate(down_w))
    hidden = first + (matmul(mixed, proj_w) + pieces[7]) + (mlp + pieces[9])
    return (hidden, (attn_in, mlp_in, query, keys, values, mixed, up_val, act))


def layer_backward(inputs, saved, mats, pieces, grad_hidden, ahead):
    query_w, kv_w, proj_w, up_w, down_w = mats
    attn_in, mlp_in, query, keys, values, mixed, up_val, act = saved
    live = inputs.shape[0] // 2
    slots = live // RESP
    first = inputs[:live]
    grad_low = grad_hidden.astype(jnp.bfloat16)
    grad_sum = jnp.sum(grad_low.astype(jnp.float32), 0)
    down_grad = core_sum(act, grad_low)
    act_grad = jnp.concatenate([matmul_nt(grad_low, part) for part in down_w], axis=1)
    gelu_out, gelu_pull = jax.vjp(gelu_exact, up_val)
    up_grad_low = gelu_pull(act_grad)[0].astype(jnp.bfloat16)
    up_w_grad = core_sum(mlp_in, up_grad_low)
    mlp_in_grad = matmul_nt(up_grad_low, up_w)
    proj_grad = core_sum(mixed, grad_low)
    mixed_grad = (
        matmul_nt(grad_low, proj_w).astype(jnp.bfloat16).reshape(slots, RESP, HEADS, HEAD_DIM)
    )
    probs = attention_probs(query, keys)
    probs_low = probs.astype(jnp.bfloat16)
    probs_grad = jnp.einsum(
        "cqhd,ckhd->chqk", mixed_grad, values, preferred_element_type=jnp.float32
    )
    value_grad = jnp.einsum(
        "chqk,cqhd->ckhd", probs_low, mixed_grad, preferred_element_type=jnp.float32
    )
    score_grad = probs * (probs_grad - jnp.sum(probs * probs_grad, -1, keepdims=True))
    score_grad = score_grad.astype(jnp.bfloat16)
    scale = HEAD_DIM ** (-0.5)
    query_grad = (
        jnp.einsum("chqk,ckhd->cqhd", score_grad, keys, preferred_element_type=jnp.float32) * scale
    )
    key_grad = (
        jnp.einsum("chqk,cqhd->ckhd", score_grad, query, preferred_element_type=jnp.float32) * scale
    )
    query_grad = rotary(query_grad, key_places()[:RESP], -1.0).reshape(live, D)
    key_grad = rotary(key_grad, key_places(), -1.0).reshape(slots, SEQ, D)
    value_grad = value_grad.reshape(slots, SEQ, D)
    query_grad = query_grad.astype(jnp.bfloat16)
    both_grad = jnp.concatenate([parted(key_grad), parted(value_grad)], axis=1).astype(jnp.bfloat16)
    qkv_w_grad = (core_sum(attn_in[:live], query_grad), core_sum(attn_in, both_grad))
    query_grad, both_grad, ahead = lax.optimization_barrier((query_grad, both_grad, ahead))
    attn_in_grad = matmul_nt(both_grad, kv_w)
    attn_in_grad = attn_in_grad + jnp.pad(matmul_nt(query_grad, query_w), ((0, live), (0, 0)))
    input_one, gain_one_grad, bias_one_grad = norm_back(inputs, pieces[0], pieces[1], attn_in_grad)
    input_two, gain_two_grad, bias_two_grad = norm_back(first, pieces[2], pieces[3], mlp_in_grad)
    input_grad = input_one + jnp.pad(grad_hidden + input_two, ((0, live), (0, 0)))
    vector_head = [gain_one_grad, bias_one_grad, gain_two_grad, bias_two_grad]
    vector_tail = [
        jnp.sum(query_grad.astype(jnp.float32), 0),
        jnp.sum(both_grad.astype(jnp.float32), 0),
        grad_sum,
        jnp.sum(up_grad_low.astype(jnp.float32), 0),
        grad_sum,
    ]
    mat_grads = (qkv_w_grad, proj_grad, up_w_grad, down_grad)
    return (input_grad, mat_grads, vector_head, vector_tail, ahead)


def pro_single(scores, weight, ranks, count):
    valid = ranks < count
    head = ranks < count - 1
    peak = jnp.max(jnp.where(valid, scores, -1e30))
    expo = jnp.where(valid, jnp.exp(scores - peak), 0.0)
    later = ranks[None, :] >= ranks[:, None]
    suffix = jnp.sum(jnp.where(later, expo[None, :], 0.0), -1)
    return jnp.sum(
        jnp.where(head, -weight * (scores - peak - jnp.log(jnp.where(head, suffix, 1.0))), 0.0)
    )


def moments(first, second, grad, factor):
    clipped = grad * factor
    first_new = BETA_ONE * first + (1.0 - BETA_ONE) * clipped
    second_new = BETA_TWO * second + (1.0 - BETA_TWO) * clipped * clipped
    return (first_new, second_new)


def adam_update(weight, first, second, grad, factor):
    first_new, second_new = moments(first, second, grad, factor)
    first_hat = first_new / (1.0 - BETA_ONE**STEP)
    second_hat = second_new / (1.0 - BETA_TWO**STEP)
    weight_new = weight - LEARN_RATE * (
        first_hat / (jnp.sqrt(second_hat) + ADAM_EPS) + DECAY * weight
    )
    return (first_new, second_new, weight_new)


def body(
    token_ids,
    token_mask,
    resp_lengths,
    cand_counts,
    cand_rank,
    rewards,
    embed_table,
    embed_first,
    embed_second,
    head_table,
    head_first,
    head_second,
    qkv_weight,
    qkv_first,
    qkv_second,
    proj_weight,
    proj_first,
    proj_second,
    up_weight,
    up_first,
    up_second,
    down_weight,
    down_first,
    down_second,
    vector_params,
    vector_first,
    vector_second,
):
    slots = token_ids.shape[1]
    rows_own = slots * RESP
    core = lax.axis_index("cand")
    here = [lax.axis_index(axis) for axis in AXES]
    vocab_local = head_table.shape[0]
    pieces = split_params(vector_params)

    everyone = ("cand", *AXES)
    me = lax.axis_index(everyone)
    quarter = me // 32
    down_low = down_weight.reshape(RING, 8, D)
    moved = []
    for step in range(RING):
        group = lax.dynamic_index_in_dim(down_low, (step + quarter) % RING, 0, False)
        moved.append(
            lax.ppermute(
                group.astype(jnp.bfloat16),
                everyone,
                [(d, RING * (d % 32) + (step + d // 32) % RING) for d in range(128)],
            ).astype(jnp.float32)
        )
    moved = jnp.stack(moved)
    down_rows = [
        lax.dynamic_index_in_dim(moved, (me - k) % RING, 0, False) for k in range(RING)
    ]
    packed = jnp.concatenate([qkv_weight, up_weight, proj_weight, *down_rows], axis=1)
    gathered = lax.all_gather(packed.astype(jnp.bfloat16), everyone, axis=0, tiled=True)
    mats = (
        gathered[:, :D],
        gathered[:, D : 3 * D],
        gathered[:, 7 * D : 8 * D],
        gathered[:, 3 * D : 7 * D],
        [gathered[:, (8 + k) * D : (9 + k) * D] for k in range(RING)],
    )

    live = (
        (jnp.arange(RESP)[None, None, :] < resp_lengths[:, :, None]) & (token_mask == 1)
    ).astype(jnp.float32)
    valid = (cand_rank < cand_counts[:, None]).astype(jnp.float32)
    top_mask = (cand_rank == 0).astype(jnp.float32)
    stats = jnp.stack(
        [
            jnp.sum(valid),
            jnp.sum(rewards * valid),
            jnp.sum(rewards * rewards * valid),
            jnp.sum(live * top_mask[..., None]),
        ]
    )

    turned = jnp.concatenate(
        [token_ids[0, :, SEQ - RESP - 1 :], token_ids[0, :, : SEQ - RESP - 1]], axis=1
    )
    posted = spread(
        jnp.concatenate([turned.reshape(-1).astype(jnp.float32), stats, jnp.zeros(60)]), AXES
    )
    all_ids = posted[:, : slots * SEQ].astype(jnp.int32)
    stats = jnp.sum(posted[:, slots * SEQ : slots * SEQ + 4], 0)
    group_ids = lax.dynamic_index_in_dim(all_ids.reshape(16, RING, slots, SEQ), here[2], 1, False)
    group_targets = group_ids[:, :, 1 : RESP + 1].reshape(-1)
    flat_ids = all_ids.reshape(64, slots, 2, RESP).transpose(0, 2, 1, 3).reshape(-1)
    looked = look_up(embed_table.T, flat_ids).astype(jnp.bfloat16)
    looked = looked.reshape(16, 64, slots * SEQ).swapaxes(0, 1)
    inputs = exchange(looked, AXES).reshape(D, slots * SEQ).T.astype(jnp.float32)

    head_low = jnp.pad(head_table.astype(jnp.bfloat16), ((0, 2 * PAD_HALF - vocab_local), (0, 0)))
    head_half = lax.dynamic_slice_in_dim(head_low, core * PAD_HALF, PAD_HALF)
    head_half, inputs = lax.optimization_barrier((head_half, inputs))
    mine = spread(head_half, "z").reshape(-1, D)

    other = swap(
        jnp.concatenate([stats, rewards.reshape(-1), cand_rank.reshape(-1).astype(jnp.float32)])
    )
    stats = stats + other[:4]
    mean = stats[1] / stats[0]
    variance = stats[2] / stats[0] - mean * mean

    def both(value, second):
        return jnp.where(
            core == 0, jnp.concatenate([value, second]), jnp.concatenate([second, value])
        )

    all_rank = both(cand_rank.reshape(-1), other[4 + slots :].astype(jnp.int32))
    all_rewards = both(rewards.reshape(-1), other[4 : 4 + slots])
    weight = jax.nn.softplus((all_rewards - mean) * lax.rsqrt(variance + NORM_EPS))

    hidden, saved = layer_forward(inputs, mats, pieces)
    rows_low = layer_norm(hidden, pieces[4], pieces[5]).astype(jnp.bfloat16)

    rows_low, mine = lax.optimization_barrier((rows_low, mine))
    group_rows = spread(rows_low, ("x", "y")).reshape(-1, D)
    head_group = jnp.concatenate([mine, swap(mine)], axis=0)

    shard = group_targets // vocab_local
    offset = group_targets % vocab_local
    part = jnp.where(offset // PAD_HALF == core, 0, 1)
    local = (shard // RING) == here[0] * RING + here[1]
    targets = jnp.where(
        local, (part * RING + shard % RING) * PAD_HALF + offset % PAD_HALF, -1
    )
    column = jnp.arange(2 * RING * PAD_HALF)[None, :]
    half = jnp.where(column < RING * PAD_HALF, core, 1 - core)
    real = half * PAD_HALF + column % PAD_HALF < vocab_local
    logits = jnp.where(real, matmul_nt(group_rows, head_group), -1e30)
    hits = column == targets[:, None]
    local_max = jnp.max(logits, -1)
    local_sum = jnp.sum(jnp.exp(logits - local_max[:, None]), -1)
    local_target = jnp.sum(jnp.where(hits, logits, 0.0), -1)

    held = jnp.stack([local_max, local_sum, local_target], axis=1).reshape(16, rows_own, 3)
    held = exchange(held.swapaxes(1, 2), ("x", "y"))
    biggest = jnp.max(held[:, 0], 0)
    held = (
        biggest,
        jnp.sum(held[:, 1] * jnp.exp(held[:, 0] - biggest), 0),
        jnp.sum(held[:, 2], 0),
    )
    row_lse = held[0] + jnp.log(held[1])
    own_logp = (held[2] - row_lse).reshape(1, slots, RESP)
    own_count = jnp.sum(live, -1)
    own_scores = jnp.sum(own_logp * live, -1) / jnp.maximum(own_count, 1.0)
    all_scores = both(own_scores.reshape(-1), swap(own_scores.reshape(-1)))
    pro_value, pro_grad = jax.value_and_grad(pro_single)(
        all_scores, weight, all_rank, cand_counts[0]
    )
    my_grad = lax.dynamic_slice_in_dim(pro_grad, core * slots, slots).reshape(1, slots)
    sft_scale = 64 / jnp.maximum(stats[3], 1.0)
    row_grad = (
        my_grad[..., None] / jnp.maximum(own_count, 1.0)[..., None]
        - sft_scale * top_mask[..., None]
    ) * live
    back = spread(jnp.stack([row_grad.reshape(-1), row_lse]), ("x", "y"))
    group_grad = back[:, 0].reshape(-1)
    group_lse = back[:, 1].reshape(-1)

    vocab_probs = jnp.exp(logits - group_lse[:, None])
    logit_grad = (group_grad[:, None] * (hits.astype(jnp.float32) - vocab_probs)).astype(
        jnp.bfloat16
    )
    rows_part = matmul(logit_grad, head_group).astype(jnp.bfloat16)
    rows_part = exchange(rows_part.reshape(16, rows_own, D), ("x", "y"))
    near = RING * PAD_HALF
    head_part = matmul_tn(logit_grad[:, :near], group_rows) + swap(
        matmul_tn(logit_grad[:, near:], group_rows).astype(jnp.bfloat16)
    ).astype(jnp.float32)
    head_part = head_part.astype(jnp.bfloat16).reshape(RING, PAD_HALF, D)
    rows_part, head_part = lax.optimization_barrier((rows_part, head_part))
    head_part = exchange(head_part, "z")
    rows_grad = jnp.sum(rows_part.astype(jnp.float32), 0)

    grad_hidden, gain_fin_grad, bias_fin_grad = norm_back(hidden, pieces[4], pieces[5], rows_grad)
    input_grad, mat_grads, vector_head, vector_tail, head_part = layer_backward(
        inputs, saved, mats, pieces, grad_hidden, head_part
    )
    head_own = jnp.sum(head_part.astype(jnp.float32), 0)

    head_grad = both(head_own, swap(head_own))[:vocab_local]

    (query_g, kv_g), proj_g, up_g, down_g = mat_grads
    vector_grad = jnp.concatenate(vector_head + [gain_fin_grad, bias_fin_grad] + vector_tail)
    vector_high = vector_grad.astype(jnp.bfloat16)
    vector_low = (vector_grad - vector_high.astype(jnp.float32)).astype(jnp.bfloat16)
    vector_both = jnp.stack([vector_high, vector_low]).reshape(4, 64, 120).swapaxes(0, 1)
    vector_both = jnp.pad(vector_both, ((0, 0), (0, 4), (0, slots * SEQ - 120)))
    turned_grad = input_grad.astype(jnp.bfloat16).T.reshape(64, 16, slots * SEQ)
    turned_grad = jnp.concatenate([turned_grad, vector_both], axis=1)
    rest = jnp.concatenate([up_g, proj_g, query_g, kv_g], axis=1).reshape(64, 8, 8 * D)
    down_g = down_g.reshape(64, 32, D)
    down_g, head_own = lax.optimization_barrier((down_g, head_own))
    down_g = exchange(down_g, AXES)
    turned_grad, down_g, rest = lax.optimization_barrier((turned_grad, down_g, rest))
    turned_grad = exchange(turned_grad, AXES)
    embed_rows = turned_grad[:, :16].astype(jnp.float32).swapaxes(0, 1).reshape(16, -1)
    vector_both = jnp.sum(turned_grad[:, 16:20, :120].astype(jnp.float32), 0).reshape(2, 2, 120)
    vector_both = vector_both[0] + vector_both[1]
    vector_grad = lax.dynamic_index_in_dim(vector_both, core, 0, False) + swap(
        lax.dynamic_index_in_dim(vector_both, 1 - core, 0, False)
    )

    rest, embed_rows = lax.optimization_barrier((rest, embed_rows))
    rest = exchange(rest, AXES)
    embed_grad = fold(embed_rows, flat_ids, embed_table.shape[0])
    embed_grad = (embed_grad + swap(embed_grad)).T
    rest = jnp.sum(rest.astype(jnp.float32), 0)

    down_g = jnp.sum(down_g.astype(jnp.float32), 0)
    shards = (rest[:, 5 * D :], rest[:, 4 * D : 5 * D], rest[:, : 4 * D], down_g, vector_grad)
    local_squares = sum((jnp.sum(piece * piece) for piece in shards))
    local_squares = (
        local_squares + (jnp.sum(embed_grad * embed_grad) + jnp.sum(head_grad * head_grad)) / 2
    )
    sft_local = -jnp.sum(own_logp * live * top_mask[..., None])
    sums = jnp.sum(
        spread(jnp.stack([local_squares, pro_value / 2, sft_local]), ("cand", *AXES)), 0
    )
    grad_norm = jnp.sqrt(sums[0])
    factor = jnp.minimum(1.0, CLIP_NORM / (grad_norm + 1e-06))
    embed_new = adam_update(embed_table, embed_first, embed_second, embed_grad, factor)
    head_new = adam_update(head_table, head_first, head_second, head_grad, factor)
    qkv_new = adam_update(qkv_weight, qkv_first, qkv_second, shards[0], factor)
    proj_new = adam_update(proj_weight, proj_first, proj_second, shards[1], factor)
    up_new = adam_update(up_weight, up_first, up_second, shards[2], factor)
    down_new = adam_update(down_weight, down_first, down_second, shards[3], factor)
    vector_first_new, vector_second_new = moments(vector_first, vector_second, shards[4], factor)
    loss_parts = jnp.stack([sums[1], sums[2], stats[3]])
    return (
        loss_parts,
        grad_norm,
        my_grad,
        embed_new[0],
        embed_new[1],
        embed_new[2],
        head_new[0],
        head_new[1],
        head_new[2],
        qkv_new[0],
        qkv_new[1],
        qkv_new[2],
        proj_new[0],
        proj_new[1],
        proj_new[2],
        up_new[0],
        up_new[1],
        up_new[2],
        down_new[0],
        down_new[1],
        down_new[2],
        vector_first_new,
        vector_second_new,
    )


def solution(mesh):
    fine = Mesh(mesh.devices.reshape(2, RING, RING, RING), ("cand", *AXES))
    in_specs = (
        P(AXES, "cand", None),
        P(AXES, "cand", None),
        P(AXES, "cand"),
        P(AXES),
        P(AXES, "cand"),
        P(AXES, "cand"),
        P(None, AXES),
        P(None, AXES),
        P(None, AXES),
        P(AXES, None),
        P(AXES, None),
        P(AXES, None),
        P(("cand", *AXES), None),
        P(("cand", *AXES), None),
        P(("cand", *AXES), None),
        P(("cand", *AXES), None),
        P(("cand", *AXES), None),
        P(("cand", *AXES), None),
        P(("cand", *AXES), None),
        P(("cand", *AXES), None),
        P(("cand", *AXES), None),
        P(("cand", *AXES), None),
        P(("cand", *AXES), None),
        P(("cand", *AXES), None),
        P(),
        P(("cand", *AXES)),
        P(("cand", *AXES)),
    )
    out_specs = (
        P(),
        P(),
        P(AXES, "cand"),
        P(None, AXES),
        P(None, AXES),
        P(None, AXES),
        P(AXES, None),
        P(AXES, None),
        P(AXES, None),
        P(("cand", *AXES), None),
        P(("cand", *AXES), None),
        P(("cand", *AXES), None),
        P(("cand", *AXES), None),
        P(("cand", *AXES), None),
        P(("cand", *AXES), None),
        P(("cand", *AXES), None),
        P(("cand", *AXES), None),
        P(("cand", *AXES), None),
        P(("cand", *AXES), None),
        P(("cand", *AXES), None),
        P(("cand", *AXES), None),
        P(("cand", *AXES)),
        P(("cand", *AXES)),
    )
    return jax.shard_map(body, mesh=fine, in_specs=in_specs, out_specs=out_specs, check_vma=False)
```

```python
import math

import jax
import jax.numpy as jnp
import numpy as np
from jax import lax
from jax.experimental import pallas as pl
from jax.experimental.pallas import tpu as pltpu
from jax.sharding import Mesh
from jax.sharding import PartitionSpec as P

D = 1024
HEADS = 16
HEAD_DIM = 64
ROT = 16
FF = 4096
SEQ = 64
STEP = 10
RESP = 32


NORM_EPS = 1e-05
CLIP_NORM = 1.0
LEARN_RATE = 0.05
BETA_ONE = 0.9
BETA_TWO = 0.999
ADAM_EPS = 1e-08
DECAY = 0.1


RING = 4
SLOTS = 3
PAD_HALF = 448
AXES = ("x", "y", "z")


def swap(value):
    return lax.ppermute(value, "cand", [(0, 1), (1, 0)])


def exchange(pieces, axes):
    return lax.all_to_all(pieces, axes, split_axis=0, concat_axis=0, tiled=True)


def spread(value, axes):
    count = lax.axis_size(axes)
    return exchange(jnp.broadcast_to(value[None], (count, *value.shape)), axes)


def shift(value, axis, step):
    return lax.ppermute(value, axis, [(i, (i + step) % RING) for i in range(RING)])


def ring_sum(pieces, axis):
    me = lax.axis_index(axis)

    def piece(step):
        return lax.dynamic_index_in_dim(pieces, (me + step) % RING, 0, False)

    got = [shift(piece(step), axis, step).astype(jnp.float32) for step in (1, 2, 3)]
    return piece(0).astype(jnp.float32) + got[1] + (got[0] + got[2])


def of_both(value):
    return jnp.concatenate([value, swap(value)], axis=0)


def half_of_both(value):
    core = lax.axis_index("cand")
    half = value.shape[1] // 2
    kept = lax.dynamic_slice_in_dim(value, core * half, half, axis=1)
    given = lax.dynamic_slice_in_dim(value, (1 - core) * half, half, axis=1)
    return jnp.concatenate([kept, swap(given)], axis=0)


WIDE = 256
LOOK_BLOCK = 1024
FOLD_BLOCK = 2048


def look_kernel(high_ref, low_ref, table_ref, out_ref, left):
    spans = table_ref.shape[1] // WIDE
    rest = table_ref.shape[1] - spans * WIDE

    @pl.when(pl.program_id(0) == 0)
    def _():
        def fill(i, carry):
            span = table_ref[:, pl.ds(pl.multiple_of(i * WIDE, WIDE), WIDE)]
            left[pl.ds(pl.multiple_of(i * 16, 16), 16), :] = span.astype(jnp.bfloat16)
            return carry

        lax.fori_loop(0, spans, fill, 0)
        if rest:
            last = table_ref[:, spans * WIDE :].astype(jnp.bfloat16)
            left[spans * 16 :, :] = jnp.concatenate(
                [last, jnp.zeros((16, WIDE - rest), jnp.bfloat16)], axis=1
            )

    block = out_ref.shape[1]
    one_hot = jnp.where(
        lax.broadcasted_iota(jnp.int32, (WIDE, block), 0) == low_ref[...], 1.0, 0.0
    ).astype(jnp.bfloat16)
    high = jnp.broadcast_to(high_ref[...], (16, block))
    total = jnp.zeros((16, block), jnp.float32)
    rows = left.shape[0] // 16
    CH = 16
    for begin in range(0, rows, CH):
        count = min(CH, rows - begin)
        part = jnp.dot(
            left[begin * 16 : (begin + count) * 16, :], one_hot, preferred_element_type=jnp.float32
        )
        for k in range(count):
            total = total + jnp.where(high == begin + k, part[k * 16 : (k + 1) * 16], 0.0)
    out_ref[...] = total.astype(out_ref.dtype)


def look_up(table, ids):
    count = ids.shape[0]
    spans = -(-table.shape[1] // WIDE)
    high = (ids // WIDE).reshape(1, count)
    low = (ids % WIDE).reshape(1, count)
    row = pl.BlockSpec((1, LOOK_BLOCK), lambda i: (0, i))
    return pl.pallas_call(
        look_kernel,
        grid=(count // LOOK_BLOCK,),
        in_specs=[row, row, pl.BlockSpec(table.shape, lambda i: (0, 0))],
        out_specs=pl.BlockSpec((16, LOOK_BLOCK), lambda i: (0, i)),
        out_shape=jax.ShapeDtypeStruct((16, count), jnp.float32),
        scratch_shapes=[pltpu.VMEM((spans * 16, WIDE), jnp.bfloat16)],
        compiler_params=pltpu.CompilerParams(vmem_limit_bytes=40 << 20),
        cost_estimate=pl.CostEstimate(flops=2 * spans * 16 * WIDE * count, bytes_accessed=table.size * 4, transcendentals=0),
        name="look_up",
    )(high, low, table)


def fold_kernel(high_ref, low_ref, grad_ref, out_ref, left, total):
    step = pl.program_id(0)
    block = grad_ref.shape[1]
    rows = left.shape[0] // 16
    grad = grad_ref[...]
    high = jnp.broadcast_to(high_ref[...], (16, block))

    def place(i, carry):
        for k in range(4):
            at = i * 4 + k
            left[pl.ds(pl.multiple_of(at * 16, 16), 16), :] = jnp.where(
                high == at, grad, 0.0
            ).astype(jnp.bfloat16)
        return carry

    lax.fori_loop(0, rows // 4, place, 0)
    for at in range(rows // 4 * 4, rows):
        left[at * 16 : at * 16 + 16, :] = jnp.where(high == at, grad, 0.0).astype(jnp.bfloat16)
    one_hot = jnp.where(
        lax.broadcasted_iota(jnp.int32, (WIDE, block), 0) == low_ref[...], 1.0, 0.0
    ).astype(jnp.bfloat16)
    part = lax.dot_general(
        left[...], one_hot, (((1,), (1,)), ((), ())), preferred_element_type=jnp.float32
    )

    @pl.when(step == 0)
    def _():
        total[...] = part

    @pl.when(step > 0)
    def _():
        total[...] += part

    @pl.when(step == pl.num_programs(0) - 1)
    def _():
        spans = out_ref.shape[1] // WIDE
        rest = out_ref.shape[1] - spans * WIDE

        def drain(i, carry):
            out_ref[:, pl.ds(pl.multiple_of(i * WIDE, WIDE), WIDE)] = total[
                pl.ds(pl.multiple_of(i * 16, 16), 16), :
            ]
            return carry

        lax.fori_loop(0, spans, drain, 0)
        if rest:
            out_ref[:, spans * WIDE :] = total[spans * 16 :, :rest]


def fold(grads, ids, size):
    count = ids.shape[0]
    spans = -(-size // WIDE)
    high = (ids // WIDE).reshape(1, count)
    low = (ids % WIDE).reshape(1, count)
    row = pl.BlockSpec((1, FOLD_BLOCK), lambda i: (0, i))
    return pl.pallas_call(
        fold_kernel,
        grid=(count // FOLD_BLOCK,),
        in_specs=[row, row, pl.BlockSpec((16, FOLD_BLOCK), lambda i: (0, i))],
        out_specs=pl.BlockSpec((16, size), lambda i: (0, 0)),
        out_shape=jax.ShapeDtypeStruct((16, size), jnp.float32),
        scratch_shapes=[
            pltpu.VMEM((spans * 16, FOLD_BLOCK), jnp.bfloat16),
            pltpu.VMEM((spans * 16, WIDE), jnp.float32),
        ],
        compiler_params=pltpu.CompilerParams(vmem_limit_bytes=40 << 20),
        cost_estimate=pl.CostEstimate(flops=2 * spans * 16 * WIDE * count, bytes_accessed=size * 64, transcendentals=0),
        name="fold",
    )(high, low, grads)


def matmul(left, right):
    return jnp.dot(left, right, preferred_element_type=jnp.float32)


def matmul_tn(left, right):
    return lax.dot_general(
        left, right, (((0,), (0,)), ((), ())), preferred_element_type=jnp.float32
    )


def matmul_nt(left, right):
    return lax.dot_general(
        left, right, (((1,), (1,)), ((), ())), preferred_element_type=jnp.float32
    )


def layer_norm(inputs, gain, bias):
    mean = jnp.mean(inputs, -1, keepdims=True)
    centred = inputs - mean
    variance = jnp.mean(centred * centred, -1, keepdims=True)
    return centred * lax.rsqrt(variance + NORM_EPS) * gain + bias


def norm_back(inputs, gain, bias, grad):
    outputs, pullback = jax.vjp(layer_norm, inputs, gain, bias)
    return pullback(grad)


def split_params(vector):
    spans = [D, D, D, D, D, D, 3 * D, D, FF, D]
    pieces = []
    begin = 0
    for span_len in spans:
        pieces.append(vector[begin : begin + span_len])
        begin = begin + span_len
    return pieces


def turn(values, tables, sign):
    cosine, low, high = tables
    return (
        values * cosine
        + sign * (pltpu.roll(values, 120, axis=1) * low + pltpu.roll(values, 8, axis=1) * high)
    )


def dot_nn(left, right):
    return jnp.dot(left, right, preferred_element_type=jnp.float32)


def dot_nt(left, right):
    return lax.dot_general(
        left, right, (((1,), (1,)), ((), ())), preferred_element_type=jnp.float32
    )


def dot_tn(left, right):
    return lax.dot_general(
        left, right, (((0,), (0,)), ((), ())), preferred_element_type=jnp.float32
    )


def pair_of(values):
    lanes = lax.broadcasted_iota(jnp.int32, values.shape, 1)
    zero = jnp.zeros_like(values)
    return (jnp.where(lanes < HEAD_DIM, values, zero), jnp.where(lanes < HEAD_DIM, zero, values))


def row_places(rows, width, axis):
    row = lax.broadcasted_iota(jnp.int32, (rows, width), axis)
    live = SLOTS * RESP
    late = row >= live
    row = jnp.where(late, row - live, row)
    inside = row % RESP
    place = jnp.where(
        late, jnp.where(inside == 0, SEQ - 1, inside - 1), inside + (SEQ - RESP - 1)
    )
    return row // RESP, place


def softmax_rows(query, keys):
    rows, width = query.shape[0], keys.shape[0]
    scores = dot_nt(query, keys) * HEAD_DIM ** (-0.5)
    query_slot, query_place = row_places(rows, width, 0)
    key_slot, key_place = row_places(rows, width, 1)
    seen = (query_slot == key_slot) & (query_place >= key_place)
    scores = jnp.where(seen, scores, -1e30)
    scores = jnp.exp(scores - jnp.max(scores, axis=1, keepdims=True))
    return scores / jnp.sum(scores, axis=1, keepdims=True)


def forward_kernel(
    attn_ref, mlp_ref, query_w, key_w, value_w, proj_w, up_w, down_w,
    query_b, key_b, value_b, up_b, regroup, cosine, low, high,
    query_ref, key_ref, value_ref, mixed_ref, up_ref, act_ref, out_ref,
):
    live = query_ref.shape[0]
    tables = (cosine[...], low[...], high[...])
    firsts = tuple(table[:live] for table in tables)
    attn = attn_ref[...]
    query = turn(dot_nn(attn[:live], query_w[...]) + query_b[...], firsts, 1.0).astype(jnp.bfloat16)
    keys = turn(dot_nn(attn, key_w[...]) + key_b[...], tables, 1.0).astype(jnp.bfloat16)
    values = (dot_nn(attn, value_w[...]) + value_b[...]).astype(jnp.bfloat16)
    query_ref[...] = query
    key_ref[...] = keys
    value_ref[...] = values
    mixed = 0.0
    for part, held in zip(pair_of(query), pair_of(values)):
        probs = softmax_rows(part, keys).astype(jnp.bfloat16)
        mixed = mixed + dot_nn(probs, held)
    mixed = mixed.astype(jnp.bfloat16)
    mixed_ref[...] = mixed
    up_val = dot_nn(mlp_ref[...], up_w[...]) + up_b[...]
    act = (0.5 * up_val * (1.0 + lax.erf(up_val * 0.5**0.5))).astype(jnp.bfloat16)
    up_ref[...] = up_val
    act_ref[...] = act
    part = dot_nn(mixed, proj_w[...])
    act = dot_nn(act, regroup[...]).astype(jnp.bfloat16)
    for k in range(4):
        part = part + dot_nn(act[:, 128 * k : 128 * k + 128], down_w[:, D * k : D * k + D])

    @pl.when(pl.program_id(0) == 0)
    def _():
        out_ref[...] = part

    @pl.when(pl.program_id(0) > 0)
    def _():
        out_ref[...] += part


def backward_kernel(
    grad_ref, query_ref, key_ref, value_ref, up_ref, query_w, key_w, value_w, proj_w, up_w, down_w,
    regroup, cosine, low, high,
    query_g, key_g, value_g, up_g, attn_g, mlp_g, query_s, key_s, value_s, up_s,
):
    live = query_ref.shape[0]
    tables = (cosine[...], low[...], high[...])
    firsts = tuple(table[:live] for table in tables)
    grad = grad_ref[...]
    query, keys, values = query_ref[...], key_ref[...], value_ref[...]
    mixed_grad = dot_nt(grad, proj_w[...]).astype(jnp.bfloat16)
    query_grad, key_grad, value_grad = 0.0, 0.0, 0.0
    for part, held, given in zip(pair_of(query), pair_of(keys), pair_of(mixed_grad)):
        probs = softmax_rows(part, keys)
        probs_grad = dot_nt(given, values)
        value_grad = value_grad + dot_tn(probs.astype(jnp.bfloat16), given)
        score_grad = probs * (probs_grad - jnp.sum(probs * probs_grad, axis=1, keepdims=True))
        score_grad = score_grad.astype(jnp.bfloat16)
        query_grad = query_grad + dot_nn(score_grad, held)
        key_grad = key_grad + dot_tn(score_grad, part)
    scale = HEAD_DIM ** (-0.5)
    query_grad = turn(query_grad * scale, firsts, -1.0).astype(jnp.bfloat16)
    key_grad = turn(key_grad * scale, tables, -1.0).astype(jnp.bfloat16)
    value_grad = value_grad.astype(jnp.bfloat16)
    act_grad = jnp.concatenate(
        [dot_nt(grad, down_w[:, D * k : D * k + D]) for k in range(4)], axis=1
    )
    act_high = act_grad.astype(jnp.bfloat16)
    act_low = (act_grad - act_high.astype(jnp.float32)).astype(jnp.bfloat16)
    act_grad = dot_nt(act_high, regroup[...]) + dot_nt(act_low, regroup[...])
    up_val = up_ref[...]
    slope = 0.5 * (1.0 + lax.erf(up_val * 0.5**0.5)) + up_val * (
        jnp.exp(-0.5 * up_val * up_val) * (2.0 * math.pi) ** (-0.5)
    )
    up_grad = (act_grad * slope).astype(jnp.bfloat16)
    for ref, sums, value in (
        (query_g, query_s, query_grad),
        (key_g, key_s, key_grad),
        (value_g, value_s, value_grad),
        (up_g, up_s, up_grad),
    ):
        ref[...] = value
        sums[...] = jnp.sum(value.astype(jnp.float32), axis=0, keepdims=True)
    first = dot_nt(query_grad, query_w[...])
    both = dot_nt(key_grad, key_w[...]) + dot_nt(value_grad, value_w[...])
    mlp = dot_nt(up_grad, up_w[...])

    @pl.when(pl.program_id(0) == 0)
    def _():
        attn_g[...] = both
        attn_g[:live] += first
        mlp_g[...] = mlp

    @pl.when(pl.program_id(0) > 0)
    def _():
        attn_g[...] += both
        attn_g[:live] += first
        mlp_g[...] += mlp


def turn_tables(slots):
    half = ROT // 2
    row = np.arange(2 * slots * RESP)
    inside = row % RESP
    place = np.where(row < slots * RESP, inside + SEQ - RESP - 1, (inside - 1) % SEQ)
    lane = np.arange(2 * HEAD_DIM) % HEAD_DIM
    freq = np.float32(10000.0) ** (-(np.arange(half) * np.float32(2.0 / ROT)).astype(np.float32))
    angle = place.astype(np.float32)[:, None] * freq.astype(np.float32)[lane % half][None, :]
    cosine = np.where(lane < ROT, np.cos(angle), 1.0).astype(np.float32)
    sine = np.sin(angle)
    low = np.where(lane < half, -sine, 0.0).astype(np.float32)
    high = np.where((lane >= half) & (lane < ROT), sine, 0.0).astype(np.float32)
    return cosine, low, high


def regroup_table():
    at = np.arange(512)
    to = (at // 8 % 4) * 128 + (at // 32) * 8 + at % 8
    table = np.zeros((512, 512), np.float32)
    table[at, to] = 1.0
    return jnp.asarray(table, jnp.bfloat16)


def weight_specs():
    wide = 2 * HEAD_DIM
    return [
        pl.BlockSpec((D, wide), lambda j: (0, j)),
        pl.BlockSpec((D, wide), lambda j: (0, 8 + j)),
        pl.BlockSpec((D, wide), lambda j: (0, 16 + j)),
        pl.BlockSpec((wide, D), lambda j: (j, 7)),
        pl.BlockSpec((D, 512), lambda j: (0, 6 + j)),
        pl.BlockSpec((128, 4 * D), lambda j: (j, 2)),
    ]


def whole(*shape):
    return pl.BlockSpec(shape, lambda j: (0, 0))


def columns(rows, width):
    return pl.BlockSpec((rows, width), lambda j: (0, j))


def layer_forward(attn_in, mlp_in, gathered, pieces, tables):
    rows, live = attn_in.shape[0], mlp_in.shape[0]
    wide = 2 * HEAD_DIM
    bias = pieces[6].reshape(1, 3 * D)
    shape = jax.ShapeDtypeStruct
    return pl.pallas_call(
        forward_kernel,
        grid=(HEADS // 2,),
        in_specs=[whole(rows, D), whole(live, D)]
        + weight_specs()
        + [
            pl.BlockSpec((1, wide), lambda j: (0, j)),
            pl.BlockSpec((1, wide), lambda j: (0, 8 + j)),
            pl.BlockSpec((1, wide), lambda j: (0, 16 + j)),
            columns(1, 512),
        ]
        + [whole(512, 512)]
        + [whole(rows, wide)] * 3,
        out_specs=[
            columns(live, wide),
            columns(rows, wide),
            columns(rows, wide),
            columns(live, wide),
            columns(live, 512),
            columns(live, 512),
            whole(live, D),
        ],
        out_shape=[
            shape((live, D), jnp.bfloat16),
            shape((rows, D), jnp.bfloat16),
            shape((rows, D), jnp.bfloat16),
            shape((live, D), jnp.bfloat16),
            shape((live, FF), jnp.float32),
            shape((live, FF), jnp.bfloat16),
            shape((live, D), jnp.float32),
        ],
        compiler_params=pltpu.CompilerParams(vmem_limit_bytes=40 << 20),
        cost_estimate=pl.CostEstimate(
            flops=2 * live * 16 * D * D, bytes_accessed=64 * D * D, transcendentals=0
        ),
        name="layer_forward",
    )(attn_in, mlp_in, *[gathered] * 6, bias, bias, bias, pieces[8].reshape(1, FF), regroup_table(), *tables)


def layer_backward(grad_low, saved, gathered, tables):
    query, keys, values, up_val = saved
    rows, live = keys.shape[0], query.shape[0]
    wide = 2 * HEAD_DIM
    shape = jax.ShapeDtypeStruct
    return pl.pallas_call(
        backward_kernel,
        grid=(HEADS // 2,),
        in_specs=[
            whole(live, D),
            columns(live, wide),
            columns(rows, wide),
            columns(rows, wide),
            columns(live, 512),
        ]
        + weight_specs()
        + [whole(512, 512)]
        + [whole(rows, wide)] * 3,
        out_specs=[
            columns(live, wide),
            columns(rows, wide),
            columns(rows, wide),
            columns(live, 512),
            whole(rows, D),
            whole(live, D),
            columns(1, wide),
            columns(1, wide),
            columns(1, wide),
            columns(1, 512),
        ],
        out_shape=[
            shape((live, D), jnp.bfloat16),
            shape((rows, D), jnp.bfloat16),
            shape((rows, D), jnp.bfloat16),
            shape((live, FF), jnp.bfloat16),
            shape((rows, D), jnp.float32),
            shape((live, D), jnp.float32),
            shape((1, D), jnp.float32),
            shape((1, D), jnp.float32),
            shape((1, D), jnp.float32),
            shape((1, FF), jnp.float32),
        ],
        compiler_params=pltpu.CompilerParams(vmem_limit_bytes=40 << 20),
        cost_estimate=pl.CostEstimate(
            flops=2 * live * 16 * D * D, bytes_accessed=64 * D * D, transcendentals=0
        ),
        name="layer_backward",
    )(grad_low, query, keys, values, up_val, *[gathered] * 6, regroup_table(), *tables)


def pro_single(scores, weight, ranks, count):
    valid = ranks < count
    head = ranks < count - 1
    peak = jnp.max(jnp.where(valid, scores, -1e30))
    expo = jnp.where(valid, jnp.exp(scores - peak), 0.0)
    later = ranks[None, :] >= ranks[:, None]
    suffix = jnp.sum(jnp.where(later, expo[None, :], 0.0), -1)
    return jnp.sum(
        jnp.where(head, -weight * (scores - peak - jnp.log(jnp.where(head, suffix, 1.0))), 0.0)
    )


def moments(first, second, grad, factor):
    clipped = grad * factor
    first_new = BETA_ONE * first + (1.0 - BETA_ONE) * clipped
    second_new = BETA_TWO * second + (1.0 - BETA_TWO) * clipped * clipped
    return (first_new, second_new)


def adam_update(weight, first, second, grad, factor):
    first_new, second_new = moments(first, second, grad, factor)
    first_hat = first_new / (1.0 - BETA_ONE**STEP)
    second_hat = second_new / (1.0 - BETA_TWO**STEP)
    weight_new = weight - LEARN_RATE * (
        first_hat / (jnp.sqrt(second_hat) + ADAM_EPS) + DECAY * weight
    )
    return (first_new, second_new, weight_new)


def body(
    token_ids,
    token_mask,
    resp_lengths,
    cand_counts,
    cand_rank,
    rewards,
    embed_table,
    embed_first,
    embed_second,
    head_table,
    head_first,
    head_second,
    qkv_weight,
    qkv_first,
    qkv_second,
    proj_weight,
    proj_first,
    proj_second,
    up_weight,
    up_first,
    up_second,
    down_weight,
    down_first,
    down_second,
    vector_params,
    vector_first,
    vector_second,
):
    slots = token_ids.shape[1]
    rows_own = slots * RESP
    core = lax.axis_index("cand")
    here = [lax.axis_index(axis) for axis in AXES]
    vocab_local = head_table.shape[0]
    pieces = split_params(vector_params)

    packed = jnp.concatenate(
        [qkv_weight, up_weight, proj_weight, *[down_weight[8 * k : 8 * k + 8] for k in range(4)]],
        axis=1,
    )
    gathered = lax.all_gather(
        packed.astype(jnp.bfloat16), ("cand", *AXES), axis=0, tiled=True
    )

    live = (
        (jnp.arange(RESP)[None, None, :] < resp_lengths[:, :, None]) & (token_mask == 1)
    ).astype(jnp.float32)
    valid = (cand_rank < cand_counts[:, None]).astype(jnp.float32)
    top_mask = (cand_rank == 0).astype(jnp.float32)
    stats = jnp.stack(
        [
            jnp.sum(valid),
            jnp.sum(rewards * valid),
            jnp.sum(rewards * rewards * valid),
            jnp.sum(live * top_mask[..., None]),
        ]
    )

    turned = jnp.concatenate(
        [token_ids[0, :, SEQ - RESP - 1 :], token_ids[0, :, : SEQ - RESP - 1]], axis=1
    )
    posted = spread(
        jnp.concatenate([turned.reshape(-1).astype(jnp.float32), stats, jnp.zeros(60)]), AXES
    )
    all_ids = posted[:, : slots * SEQ].astype(jnp.int32)
    stats = jnp.sum(posted[:, slots * SEQ : slots * SEQ + 4], 0)
    group_ids = lax.dynamic_index_in_dim(all_ids.reshape(16, RING, slots, SEQ), here[2], 1, False)
    group_targets = group_ids[:, :, 1 : RESP + 1].reshape(-1)
    flat_ids = all_ids.reshape(64, slots, 2, RESP).transpose(0, 2, 1, 3).reshape(-1)
    looked = look_up(embed_table.T, flat_ids).astype(jnp.bfloat16)
    looked = looked.reshape(16, 64, slots * SEQ).swapaxes(0, 1)
    inputs = exchange(looked, AXES).reshape(D, slots * SEQ).T.astype(jnp.float32)

    head_low = jnp.pad(head_table.astype(jnp.bfloat16), ((0, 2 * PAD_HALF - vocab_local), (0, 0)))
    head_half = lax.dynamic_slice_in_dim(head_low, core * PAD_HALF, PAD_HALF)
    head_half, inputs = lax.optimization_barrier((head_half, inputs))
    mine = spread(head_half, "z").reshape(-1, D)

    other = swap(
        jnp.concatenate([stats, rewards.reshape(-1), cand_rank.reshape(-1).astype(jnp.float32)])
    )
    stats = stats + other[:4]
    mean = stats[1] / stats[0]
    variance = stats[2] / stats[0] - mean * mean

    def both(value, second):
        return jnp.where(
            core == 0, jnp.concatenate([value, second]), jnp.concatenate([second, value])
        )

    all_rank = both(cand_rank.reshape(-1), other[4 + slots :].astype(jnp.int32))
    all_rewards = both(rewards.reshape(-1), other[4 : 4 + slots])
    weight = jax.nn.softplus((all_rewards - mean) * lax.rsqrt(variance + NORM_EPS))

    live_rows = slots * RESP
    first_rows = inputs[:live_rows]
    attn_in = layer_norm(inputs, pieces[0], pieces[1]).astype(jnp.bfloat16)
    mlp_in = layer_norm(first_rows, pieces[2], pieces[3]).astype(jnp.bfloat16)
    tables = turn_tables(slots)
    query, keys, values, mixed, up_val, act, added = layer_forward(
        attn_in, mlp_in, gathered, pieces, tables
    )
    hidden = first_rows + added + (pieces[7] + pieces[9])
    rows_low = layer_norm(hidden, pieces[4], pieces[5]).astype(jnp.bfloat16)

    rows_low, mine = lax.optimization_barrier((rows_low, mine))
    group_rows = spread(rows_low, ("x", "y")).reshape(-1, D)
    head_group = jnp.concatenate([mine, swap(mine)], axis=0)

    shard = group_targets // vocab_local
    offset = group_targets % vocab_local
    part = jnp.where(offset // PAD_HALF == core, 0, 1)
    local = (shard // RING) == here[0] * RING + here[1]
    targets = jnp.where(
        local, (part * RING + shard % RING) * PAD_HALF + offset % PAD_HALF, -1
    )
    column = jnp.arange(2 * RING * PAD_HALF)[None, :]
    half = jnp.where(column < RING * PAD_HALF, core, 1 - core)
    real = half * PAD_HALF + column % PAD_HALF < vocab_local
    logits = jnp.where(real, matmul_nt(group_rows, head_group), -1e30)
    hits = column == targets[:, None]
    local_max = jnp.max(logits, -1)
    local_sum = jnp.sum(jnp.exp(logits - local_max[:, None]), -1)
    local_target = jnp.sum(jnp.where(hits, logits, 0.0), -1)

    held = jnp.stack([local_max, local_sum, local_target], axis=1).reshape(16, rows_own, 3)
    held = exchange(held.swapaxes(1, 2), ("x", "y"))
    biggest = jnp.max(held[:, 0], 0)
    held = (
        biggest,
        jnp.sum(held[:, 1] * jnp.exp(held[:, 0] - biggest), 0),
        jnp.sum(held[:, 2], 0),
    )
    row_lse = held[0] + jnp.log(held[1])
    own_logp = (held[2] - row_lse).reshape(1, slots, RESP)
    own_count = jnp.sum(live, -1)
    own_scores = jnp.sum(own_logp * live, -1) / jnp.maximum(own_count, 1.0)
    all_scores = both(own_scores.reshape(-1), swap(own_scores.reshape(-1)))
    pro_value, pro_grad = jax.value_and_grad(pro_single)(
        all_scores, weight, all_rank, cand_counts[0]
    )
    my_grad = lax.dynamic_slice_in_dim(pro_grad, core * slots, slots).reshape(1, slots)
    sft_scale = 64 / jnp.maximum(stats[3], 1.0)
    row_grad = (
        my_grad[..., None] / jnp.maximum(own_count, 1.0)[..., None]
        - sft_scale * top_mask[..., None]
    ) * live
    back = spread(jnp.stack([row_grad.reshape(-1), row_lse]), ("x", "y"))
    group_grad = back[:, 0].reshape(-1)
    group_lse = back[:, 1].reshape(-1)

    vocab_probs = jnp.exp(logits - group_lse[:, None])
    logit_grad = (group_grad[:, None] * (hits.astype(jnp.float32) - vocab_probs)).astype(
        jnp.bfloat16
    )
    rows_part = matmul(logit_grad, head_group).astype(jnp.bfloat16)
    rows_part = exchange(rows_part.reshape(16, rows_own, D), ("x", "y"))
    near = RING * PAD_HALF
    head_part = matmul_tn(logit_grad[:, :near], group_rows) + swap(
        matmul_tn(logit_grad[:, near:], group_rows).astype(jnp.bfloat16)
    ).astype(jnp.float32)
    head_part = head_part.astype(jnp.bfloat16).reshape(RING, PAD_HALF, D)
    rows_part, head_part = lax.optimization_barrier((rows_part, head_part))
    head_own = ring_sum(head_part, "z")
    rows_grad = jnp.sum(rows_part.astype(jnp.float32), 0)

    grad_hidden, gain_fin_grad, bias_fin_grad = norm_back(hidden, pieces[4], pieces[5], rows_grad)
    grad_low = grad_hidden.astype(jnp.bfloat16)
    grad_sum = jnp.sum(grad_low.astype(jnp.float32), 0)
    grad_both = of_both(grad_low)
    down_g = matmul_tn(half_of_both(act), grad_both).astype(jnp.bfloat16).reshape(64, 32, D)
    down_g = exchange(down_g, AXES)
    query_grad, key_grad, value_grad, up_grad, attn_grad, mlp_grad, *sums = layer_backward(
        grad_low, (query, keys, values, up_val), gathered, tables
    )
    attn_grad, mlp_grad, down_g = lax.optimization_barrier((attn_grad, mlp_grad, down_g))
    input_one, gain_one_grad, bias_one_grad = norm_back(inputs, pieces[0], pieces[1], attn_grad)
    input_two, gain_two_grad, bias_two_grad = norm_back(first_rows, pieces[2], pieces[3], mlp_grad)
    input_grad = input_one + jnp.pad(grad_hidden + input_two, ((0, live_rows), (0, 0)))
    attn_both = half_of_both(attn_in)
    first_both = jnp.concatenate(
        [attn_both[:live_rows], attn_both[2 * live_rows : 3 * live_rows]], axis=0
    )
    up_g = matmul_tn(half_of_both(mlp_in), of_both(up_grad)).astype(jnp.bfloat16)
    proj_g = matmul_tn(half_of_both(mixed), grad_both).astype(jnp.bfloat16)
    query_g = matmul_tn(first_both, of_both(query_grad)).astype(jnp.bfloat16)
    key_g = matmul_tn(attn_both, of_both(key_grad)).astype(jnp.bfloat16)
    value_g = matmul_tn(attn_both, of_both(value_grad)).astype(jnp.bfloat16)
    vector_head = [gain_one_grad, bias_one_grad, gain_two_grad, bias_two_grad]
    vector_tail = [*[part[0] for part in sums[:3]], grad_sum, sums[3][0], grad_sum]

    head_grad = both(head_own, swap(head_own))[:vocab_local]

    vector_grad = jnp.concatenate(vector_head + [gain_fin_grad, bias_fin_grad] + vector_tail)
    vector_high = vector_grad.astype(jnp.bfloat16)
    vector_low = (vector_grad - vector_high.astype(jnp.float32)).astype(jnp.bfloat16)
    vector_both = jnp.stack([vector_high, vector_low]).reshape(4, 64, 120).swapaxes(0, 1)
    vector_both = jnp.pad(vector_both, ((0, 0), (0, 4), (0, slots * SEQ - 120)))
    turned_grad = input_grad.astype(jnp.bfloat16).T.reshape(64, 16, slots * SEQ)
    turned_grad = jnp.concatenate([turned_grad, vector_both], axis=1)
    rest = jnp.concatenate([up_g, proj_g, query_g, key_g, value_g], axis=1).reshape(64, 8, 8 * D)
    turned_grad = exchange(turned_grad, AXES)
    embed_rows = turned_grad[:, :16].astype(jnp.float32).swapaxes(0, 1).reshape(16, -1)
    vector_both = jnp.sum(turned_grad[:, 16:20, :120].astype(jnp.float32), 0).reshape(2, 2, 120)
    vector_both = vector_both[0] + vector_both[1]
    vector_grad = lax.dynamic_index_in_dim(vector_both, core, 0, False) + swap(
        lax.dynamic_index_in_dim(vector_both, 1 - core, 0, False)
    )

    rest, embed_rows = lax.optimization_barrier((rest, embed_rows))
    rest = exchange(rest, AXES)
    embed_rows, head_own = lax.optimization_barrier((embed_rows, head_own))
    embed_grad = fold(embed_rows, flat_ids, embed_table.shape[0])
    embed_grad = (embed_grad + swap(embed_grad)).T
    rest = jnp.sum(rest.astype(jnp.float32), 0)

    down_g = jnp.sum(down_g.astype(jnp.float32), 0)
    shards = (rest[:, 5 * D :], rest[:, 4 * D : 5 * D], rest[:, : 4 * D], down_g, vector_grad)
    local_squares = sum((jnp.sum(piece * piece) for piece in shards))
    local_squares = (
        local_squares + (jnp.sum(embed_grad * embed_grad) + jnp.sum(head_grad * head_grad)) / 2
    )
    sft_local = -jnp.sum(own_logp * live * top_mask[..., None])
    sums = jnp.sum(
        spread(jnp.stack([local_squares, pro_value / 2, sft_local]), ("cand", *AXES)), 0
    )
    grad_norm = jnp.sqrt(sums[0])
    factor = jnp.minimum(1.0, CLIP_NORM / (grad_norm + 1e-06))
    embed_new = adam_update(embed_table, embed_first, embed_second, embed_grad, factor)
    head_new = adam_update(head_table, head_first, head_second, head_grad, factor)
    qkv_new = adam_update(qkv_weight, qkv_first, qkv_second, shards[0], factor)
    proj_new = adam_update(proj_weight, proj_first, proj_second, shards[1], factor)
    up_new = adam_update(up_weight, up_first, up_second, shards[2], factor)
    down_new = adam_update(down_weight, down_first, down_second, shards[3], factor)
    vector_first_new, vector_second_new = moments(vector_first, vector_second, shards[4], factor)
    loss_parts = jnp.stack([sums[1], sums[2], stats[3]])
    return (
        loss_parts,
        grad_norm,
        my_grad,
        embed_new[0],
        embed_new[1],
        embed_new[2],
        head_new[0],
        head_new[1],
        head_new[2],
        qkv_new[0],
        qkv_new[1],
        qkv_new[2],
        proj_new[0],
        proj_new[1],
        proj_new[2],
        up_new[0],
        up_new[1],
        up_new[2],
        down_new[0],
        down_new[1],
        down_new[2],
        vector_first_new,
        vector_second_new,
    )


def solution(mesh):
    fine = Mesh(mesh.devices.reshape(2, RING, RING, RING), ("cand", *AXES))
    in_specs = (
        P(AXES, "cand", None),
        P(AXES, "cand", None),
        P(AXES, "cand"),
        P(AXES),
        P(AXES, "cand"),
        P(AXES, "cand"),
        P(None, AXES),
        P(None, AXES),
        P(None, AXES),
        P(AXES, None),
        P(AXES, None),
        P(AXES, None),
        P(("cand", *AXES), None),
        P(("cand", *AXES), None),
        P(("cand", *AXES), None),
        P(("cand", *AXES), None),
        P(("cand", *AXES), None),
        P(("cand", *AXES), None),
        P(("cand", *AXES), None),
        P(("cand", *AXES), None),
        P(("cand", *AXES), None),
        P(("cand", *AXES), None),
        P(("cand", *AXES), None),
        P(("cand", *AXES), None),
        P(),
        P(("cand", *AXES)),
        P(("cand", *AXES)),
    )
    out_specs = (
        P(),
        P(),
        P(AXES, "cand"),
        P(None, AXES),
        P(None, AXES),
        P(None, AXES),
        P(AXES, None),
        P(AXES, None),
        P(AXES, None),
        P(("cand", *AXES), None),
        P(("cand", *AXES), None),
        P(("cand", *AXES), None),
        P(("cand", *AXES), None),
        P(("cand", *AXES), None),
        P(("cand", *AXES), None),
        P(("cand", *AXES), None),
        P(("cand", *AXES), None),
        P(("cand", *AXES), None),
        P(("cand", *AXES), None),
        P(("cand", *AXES), None),
        P(("cand", *AXES), None),
        P(("cand", *AXES)),
        P(("cand", *AXES)),
    )
    return jax.shard_map(body, mesh=fine, in_specs=in_specs, out_specs=out_specs, check_vma=False)
```

```python
import math

import jax
import jax.numpy as jnp
import numpy as np
from jax import lax
from jax.experimental import pallas as pl
from jax.experimental.pallas import tpu as pltpu
from jax.sharding import Mesh
from jax.sharding import PartitionSpec as P

D = 1024
HEADS = 16
HEAD_DIM = 64
ROT = 16
FF = 4096
SEQ = 64
STEP = 10
RESP = 32


NORM_EPS = 1e-05
CLIP_NORM = 1.0
LEARN_RATE = 0.05
BETA_ONE = 0.9
BETA_TWO = 0.999
ADAM_EPS = 1e-08
DECAY = 0.1


RING = 4
SLOTS = 3
PAD_HALF = 448
AXES = ("x", "y", "z")


def swap(value):
    return lax.ppermute(value, "cand", [(0, 1), (1, 0)])


def exchange(pieces, axes):
    return lax.all_to_all(pieces, axes, split_axis=0, concat_axis=0, tiled=True)


def spread(value, axes):
    count = lax.axis_size(axes)
    return exchange(jnp.broadcast_to(value[None], (count, *value.shape)), axes)


def shift(value, axis, step):
    return lax.ppermute(value, axis, [(i, (i + step) % RING) for i in range(RING)])


def ring_sum(pieces, axis):
    me = lax.axis_index(axis)

    def piece(step):
        return lax.dynamic_index_in_dim(pieces, (me + step) % RING, 0, False)

    got = [shift(piece(step), axis, step).astype(jnp.float32) for step in (1, 2, 3)]
    return piece(0).astype(jnp.float32) + got[1] + (got[0] + got[2])


def of_both(value):
    return jnp.concatenate([value, swap(value)], axis=0)


def half_of_both(value):
    core = lax.axis_index("cand")
    half = value.shape[1] // 2
    kept = lax.dynamic_slice_in_dim(value, core * half, half, axis=1)
    given = lax.dynamic_slice_in_dim(value, (1 - core) * half, half, axis=1)
    return jnp.concatenate([kept, swap(given)], axis=0)


WIDE = 256
LOOK_BLOCK = 1024
FOLD_BLOCK = 2048


def look_kernel(high_ref, low_ref, table_ref, out_ref, left):
    spans = table_ref.shape[1] // WIDE
    rest = table_ref.shape[1] - spans * WIDE

    @pl.when(pl.program_id(0) == 0)
    def _():
        def fill(i, carry):
            span = table_ref[:, pl.ds(pl.multiple_of(i * WIDE, WIDE), WIDE)]
            left[pl.ds(pl.multiple_of(i * 16, 16), 16), :] = span.astype(jnp.bfloat16)
            return carry

        lax.fori_loop(0, spans, fill, 0)
        if rest:
            last = table_ref[:, spans * WIDE :].astype(jnp.bfloat16)
            left[spans * 16 :, :] = jnp.concatenate(
                [last, jnp.zeros((16, WIDE - rest), jnp.bfloat16)], axis=1
            )

    block = out_ref.shape[1]
    one_hot = jnp.where(
        lax.broadcasted_iota(jnp.int32, (WIDE, block), 0) == low_ref[...], 1.0, 0.0
    ).astype(jnp.bfloat16)
    high = jnp.broadcast_to(high_ref[...], (16, block))
    total = jnp.zeros((16, block), jnp.float32)
    rows = left.shape[0] // 16
    CH = 16
    for begin in range(0, rows, CH):
        count = min(CH, rows - begin)
        part = jnp.dot(
            left[begin * 16 : (begin + count) * 16, :], one_hot, preferred_element_type=jnp.float32
        )
        for k in range(count):
            total = total + jnp.where(high == begin + k, part[k * 16 : (k + 1) * 16], 0.0)
    out_ref[...] = total.astype(out_ref.dtype)


def look_up(table, ids):
    count = ids.shape[0]
    spans = -(-table.shape[1] // WIDE)
    high = (ids // WIDE).reshape(1, count)
    low = (ids % WIDE).reshape(1, count)
    row = pl.BlockSpec((1, LOOK_BLOCK), lambda i: (0, i))
    return pl.pallas_call(
        look_kernel,
        grid=(count // LOOK_BLOCK,),
        in_specs=[row, row, pl.BlockSpec(table.shape, lambda i: (0, 0))],
        out_specs=pl.BlockSpec((16, LOOK_BLOCK), lambda i: (0, i)),
        out_shape=jax.ShapeDtypeStruct((16, count), jnp.float32),
        scratch_shapes=[pltpu.VMEM((spans * 16, WIDE), jnp.bfloat16)],
        compiler_params=pltpu.CompilerParams(vmem_limit_bytes=40 << 20),
        cost_estimate=pl.CostEstimate(flops=2 * spans * 16 * WIDE * count, bytes_accessed=table.size * 4, transcendentals=0),
        name="look_up",
    )(high, low, table)


def fold_kernel(high_ref, low_ref, grad_ref, out_ref, left, total):
    step = pl.program_id(0)
    block = grad_ref.shape[1]
    rows = left.shape[0] // 16
    grad = grad_ref[...]
    high = jnp.broadcast_to(high_ref[...], (16, block))

    def place(i, carry):
        for k in range(4):
            at = i * 4 + k
            left[pl.ds(pl.multiple_of(at * 16, 16), 16), :] = jnp.where(
                high == at, grad, 0.0
            ).astype(jnp.bfloat16)
        return carry

    lax.fori_loop(0, rows // 4, place, 0)
    for at in range(rows // 4 * 4, rows):
        left[at * 16 : at * 16 + 16, :] = jnp.where(high == at, grad, 0.0).astype(jnp.bfloat16)
    one_hot = jnp.where(
        lax.broadcasted_iota(jnp.int32, (WIDE, block), 0) == low_ref[...], 1.0, 0.0
    ).astype(jnp.bfloat16)
    part = lax.dot_general(
        left[...], one_hot, (((1,), (1,)), ((), ())), preferred_element_type=jnp.float32
    )

    @pl.when(step == 0)
    def _():
        total[...] = part

    @pl.when(step > 0)
    def _():
        total[...] += part

    @pl.when(step == pl.num_programs(0) - 1)
    def _():
        spans = out_ref.shape[1] // WIDE
        rest = out_ref.shape[1] - spans * WIDE

        def drain(i, carry):
            out_ref[:, pl.ds(pl.multiple_of(i * WIDE, WIDE), WIDE)] = total[
                pl.ds(pl.multiple_of(i * 16, 16), 16), :
            ]
            return carry

        lax.fori_loop(0, spans, drain, 0)
        if rest:
            out_ref[:, spans * WIDE :] = total[spans * 16 :, :rest]


def fold(grads, ids, size):
    count = ids.shape[0]
    spans = -(-size // WIDE)
    high = (ids // WIDE).reshape(1, count)
    low = (ids % WIDE).reshape(1, count)
    row = pl.BlockSpec((1, FOLD_BLOCK), lambda i: (0, i))
    return pl.pallas_call(
        fold_kernel,
        grid=(count // FOLD_BLOCK,),
        in_specs=[row, row, pl.BlockSpec((16, FOLD_BLOCK), lambda i: (0, i))],
        out_specs=pl.BlockSpec((16, size), lambda i: (0, 0)),
        out_shape=jax.ShapeDtypeStruct((16, size), jnp.float32),
        scratch_shapes=[
            pltpu.VMEM((spans * 16, FOLD_BLOCK), jnp.bfloat16),
            pltpu.VMEM((spans * 16, WIDE), jnp.float32),
        ],
        compiler_params=pltpu.CompilerParams(vmem_limit_bytes=40 << 20),
        cost_estimate=pl.CostEstimate(flops=2 * spans * 16 * WIDE * count, bytes_accessed=size * 64, transcendentals=0),
        name="fold",
    )(high, low, grads)


def matmul(left, right):
    return jnp.dot(left, right, preferred_element_type=jnp.float32)


def matmul_tn(left, right):
    return lax.dot_general(
        left, right, (((0,), (0,)), ((), ())), preferred_element_type=jnp.float32
    )


def matmul_nt(left, right):
    return lax.dot_general(
        left, right, (((1,), (1,)), ((), ())), preferred_element_type=jnp.float32
    )


def layer_norm(inputs, gain, bias):
    mean = jnp.mean(inputs, -1, keepdims=True)
    centred = inputs - mean
    variance = jnp.mean(centred * centred, -1, keepdims=True)
    return centred * lax.rsqrt(variance + NORM_EPS) * gain + bias


def norm_back(inputs, gain, bias, grad):
    outputs, pullback = jax.vjp(layer_norm, inputs, gain, bias)
    return pullback(grad)


def split_params(vector):
    spans = [D, D, D, D, D, D, 3 * D, D, FF, D]
    pieces = []
    begin = 0
    for span_len in spans:
        pieces.append(vector[begin : begin + span_len])
        begin = begin + span_len
    return pieces


def turn(values, tables, sign):
    cosine, low, high = tables
    return (
        values * cosine
        + sign * (pltpu.roll(values, 120, axis=1) * low + pltpu.roll(values, 8, axis=1) * high)
    )


def dot_nn(left, right):
    return jnp.dot(left, right, preferred_element_type=jnp.float32)


def dot_nt(left, right):
    return lax.dot_general(
        left, right, (((1,), (1,)), ((), ())), preferred_element_type=jnp.float32
    )


def dot_tn(left, right):
    return lax.dot_general(
        left, right, (((0,), (0,)), ((), ())), preferred_element_type=jnp.float32
    )


def pair_of(values):
    lanes = lax.broadcasted_iota(jnp.int32, values.shape, 1)
    zero = jnp.zeros_like(values)
    return (jnp.where(lanes < HEAD_DIM, values, zero), jnp.where(lanes < HEAD_DIM, zero, values))


def row_places(rows, width, axis):
    row = lax.broadcasted_iota(jnp.int32, (rows, width), axis)
    live = SLOTS * RESP
    late = row >= live
    row = jnp.where(late, row - live, row)
    inside = row % RESP
    place = jnp.where(
        late, jnp.where(inside == 0, SEQ - 1, inside - 1), inside + (SEQ - RESP - 1)
    )
    return row // RESP, place


def softmax_rows(query, keys):
    rows, width = query.shape[0], keys.shape[0]
    scores = dot_nt(query, keys) * HEAD_DIM ** (-0.5)
    query_slot, query_place = row_places(rows, width, 0)
    key_slot, key_place = row_places(rows, width, 1)
    seen = (query_slot == key_slot) & (query_place >= key_place)
    scores = jnp.where(seen, scores, -1e30)
    scores = jnp.exp(scores - jnp.max(scores, axis=1, keepdims=True))
    return scores / jnp.sum(scores, axis=1, keepdims=True)


def forward_kernel(
    attn_ref, mlp_ref, query_w, key_w, value_w, proj_w, up_w, down_w,
    query_b, key_b, value_b, up_b, regroup, cosine, low, high,
    query_ref, key_ref, value_ref, mixed_ref, up_ref, act_ref, out_ref,
):
    live = query_ref.shape[0]
    tables = (cosine[...], low[...], high[...])
    firsts = tuple(table[:live] for table in tables)
    attn = attn_ref[...]
    query = turn(dot_nn(attn[:live], query_w[...]) + query_b[...], firsts, 1.0).astype(jnp.bfloat16)
    keys = turn(dot_nn(attn, key_w[...]) + key_b[...], tables, 1.0).astype(jnp.bfloat16)
    values = (dot_nn(attn, value_w[...]) + value_b[...]).astype(jnp.bfloat16)
    query_ref[...] = query
    key_ref[...] = keys
    value_ref[...] = values
    mixed = 0.0
    for part, held in zip(pair_of(query), pair_of(values)):
        probs = softmax_rows(part, keys).astype(jnp.bfloat16)
        mixed = mixed + dot_nn(probs, held)
    mixed = mixed.astype(jnp.bfloat16)
    mixed_ref[...] = mixed
    up_val = dot_nn(mlp_ref[...], up_w[...]) + up_b[...]
    act = (0.5 * up_val * (1.0 + lax.erf(up_val * 0.5**0.5))).astype(jnp.bfloat16)
    up_ref[...] = up_val
    act_ref[...] = act
    part = dot_nn(mixed, proj_w[...])
    act = dot_nn(act, regroup[...]).astype(jnp.bfloat16)
    for k in range(4):
        part = part + dot_nn(act[:, 128 * k : 128 * k + 128], down_w[:, D * k : D * k + D])

    @pl.when(pl.program_id(0) == 0)
    def _():
        out_ref[...] = part

    @pl.when(pl.program_id(0) > 0)
    def _():
        out_ref[...] += part


def backward_kernel(
    grad_ref, query_ref, key_ref, value_ref, up_ref, query_w, key_w, value_w, proj_w, up_w, down_w,
    regroup, cosine, low, high,
    query_g, key_g, value_g, up_g, attn_g, mlp_g, query_s, key_s, value_s, up_s,
):
    live = query_ref.shape[0]
    tables = (cosine[...], low[...], high[...])
    firsts = tuple(table[:live] for table in tables)
    grad = grad_ref[...]
    query, keys, values = query_ref[...], key_ref[...], value_ref[...]
    mixed_grad = dot_nt(grad, proj_w[...]).astype(jnp.bfloat16)
    query_grad, key_grad, value_grad = 0.0, 0.0, 0.0
    for part, held, given in zip(pair_of(query), pair_of(keys), pair_of(mixed_grad)):
        probs = softmax_rows(part, keys)
        probs_grad = dot_nt(given, values)
        value_grad = value_grad + dot_tn(probs.astype(jnp.bfloat16), given)
        score_grad = probs * (probs_grad - jnp.sum(probs * probs_grad, axis=1, keepdims=True))
        score_grad = score_grad.astype(jnp.bfloat16)
        query_grad = query_grad + dot_nn(score_grad, held)
        key_grad = key_grad + dot_tn(score_grad, part)
    scale = HEAD_DIM ** (-0.5)
    query_grad = turn(query_grad * scale, firsts, -1.0).astype(jnp.bfloat16)
    key_grad = turn(key_grad * scale, tables, -1.0).astype(jnp.bfloat16)
    value_grad = value_grad.astype(jnp.bfloat16)
    act_grad = jnp.concatenate(
        [dot_nt(grad, down_w[:, D * k : D * k + D]) for k in range(4)], axis=1
    )
    act_high = act_grad.astype(jnp.bfloat16)
    act_low = (act_grad - act_high.astype(jnp.float32)).astype(jnp.bfloat16)
    act_grad = dot_nt(act_high, regroup[...]) + dot_nt(act_low, regroup[...])
    up_val = up_ref[...]
    slope = 0.5 * (1.0 + lax.erf(up_val * 0.5**0.5)) + up_val * (
        jnp.exp(-0.5 * up_val * up_val) * (2.0 * math.pi) ** (-0.5)
    )
    up_grad = (act_grad * slope).astype(jnp.bfloat16)
    for ref, sums, value in (
        (query_g, query_s, query_grad),
        (key_g, key_s, key_grad),
        (value_g, value_s, value_grad),
        (up_g, up_s, up_grad),
    ):
        ref[...] = value
        sums[...] = jnp.sum(value.astype(jnp.float32), axis=0, keepdims=True)
    first = dot_nt(query_grad, query_w[...])
    both = dot_nt(key_grad, key_w[...]) + dot_nt(value_grad, value_w[...])
    mlp = dot_nt(up_grad, up_w[...])

    @pl.when(pl.program_id(0) == 0)
    def _():
        attn_g[...] = both
        attn_g[:live] += first
        mlp_g[...] = mlp

    @pl.when(pl.program_id(0) > 0)
    def _():
        attn_g[...] += both
        attn_g[:live] += first
        mlp_g[...] += mlp


def turn_tables(slots):
    half = ROT // 2
    row = np.arange(2 * slots * RESP)
    inside = row % RESP
    place = np.where(row < slots * RESP, inside + SEQ - RESP - 1, (inside - 1) % SEQ)
    lane = np.arange(2 * HEAD_DIM) % HEAD_DIM
    freq = np.float32(10000.0) ** (-(np.arange(half) * np.float32(2.0 / ROT)).astype(np.float32))
    angle = place.astype(np.float32)[:, None] * freq.astype(np.float32)[lane % half][None, :]
    cosine = np.where(lane < ROT, np.cos(angle), 1.0).astype(np.float32)
    sine = np.sin(angle)
    low = np.where(lane < half, -sine, 0.0).astype(np.float32)
    high = np.where((lane >= half) & (lane < ROT), sine, 0.0).astype(np.float32)
    return cosine, low, high


def regroup_table():
    at = np.arange(512)
    to = (at // 8 % 4) * 128 + (at // 32) * 8 + at % 8
    table = np.zeros((512, 512), np.float32)
    table[at, to] = 1.0
    return jnp.asarray(table, jnp.bfloat16)


def weight_specs():
    wide = 2 * HEAD_DIM
    return [
        pl.BlockSpec((D, wide), lambda j: (0, j)),
        pl.BlockSpec((D, wide), lambda j: (0, 8 + j)),
        pl.BlockSpec((D, wide), lambda j: (0, 16 + j)),
        pl.BlockSpec((wide, D), lambda j: (j, 7)),
        pl.BlockSpec((D, 512), lambda j: (0, 6 + j)),
        pl.BlockSpec((128, 4 * D), lambda j: (j, 2)),
    ]


def whole(*shape):
    return pl.BlockSpec(shape, lambda j: (0, 0))


def columns(rows, width):
    return pl.BlockSpec((rows, width), lambda j: (0, j))


def layer_forward(attn_in, mlp_in, gathered, pieces, tables):
    rows, live = attn_in.shape[0], mlp_in.shape[0]
    wide = 2 * HEAD_DIM
    bias = pieces[6].reshape(1, 3 * D)
    shape = jax.ShapeDtypeStruct
    return pl.pallas_call(
        forward_kernel,
        grid=(HEADS // 2,),
        in_specs=[whole(rows, D), whole(live, D)]
        + weight_specs()
        + [
            pl.BlockSpec((1, wide), lambda j: (0, j)),
            pl.BlockSpec((1, wide), lambda j: (0, 8 + j)),
            pl.BlockSpec((1, wide), lambda j: (0, 16 + j)),
            columns(1, 512),
        ]
        + [whole(512, 512)]
        + [whole(rows, wide)] * 3,
        out_specs=[
            columns(live, wide),
            columns(rows, wide),
            columns(rows, wide),
            columns(live, wide),
            columns(live, 512),
            columns(live, 512),
            whole(live, D),
        ],
        out_shape=[
            shape((live, D), jnp.bfloat16),
            shape((rows, D), jnp.bfloat16),
            shape((rows, D), jnp.bfloat16),
            shape((live, D), jnp.bfloat16),
            shape((live, FF), jnp.float32),
            shape((live, FF), jnp.bfloat16),
            shape((live, D), jnp.float32),
        ],
        compiler_params=pltpu.CompilerParams(vmem_limit_bytes=40 << 20),
        cost_estimate=pl.CostEstimate(
            flops=2 * live * 16 * D * D, bytes_accessed=64 * D * D, transcendentals=0
        ),
        name="layer_forward",
    )(attn_in, mlp_in, *[gathered] * 6, bias, bias, bias, pieces[8].reshape(1, FF), regroup_table(), *tables)


def layer_backward(grad_low, saved, gathered, tables):
    query, keys, values, up_val = saved
    rows, live = keys.shape[0], query.shape[0]
    wide = 2 * HEAD_DIM
    shape = jax.ShapeDtypeStruct
    return pl.pallas_call(
        backward_kernel,
        grid=(HEADS // 2,),
        in_specs=[
            whole(live, D),
            columns(live, wide),
            columns(rows, wide),
            columns(rows, wide),
            columns(live, 512),
        ]
        + weight_specs()
        + [whole(512, 512)]
        + [whole(rows, wide)] * 3,
        out_specs=[
            columns(live, wide),
            columns(rows, wide),
            columns(rows, wide),
            columns(live, 512),
            whole(rows, D),
            whole(live, D),
            columns(1, wide),
            columns(1, wide),
            columns(1, wide),
            columns(1, 512),
        ],
        out_shape=[
            shape((live, D), jnp.bfloat16),
            shape((rows, D), jnp.bfloat16),
            shape((rows, D), jnp.bfloat16),
            shape((live, FF), jnp.bfloat16),
            shape((rows, D), jnp.float32),
            shape((live, D), jnp.float32),
            shape((1, D), jnp.float32),
            shape((1, D), jnp.float32),
            shape((1, D), jnp.float32),
            shape((1, FF), jnp.float32),
        ],
        compiler_params=pltpu.CompilerParams(vmem_limit_bytes=40 << 20),
        cost_estimate=pl.CostEstimate(
            flops=2 * live * 16 * D * D, bytes_accessed=64 * D * D, transcendentals=0
        ),
        name="layer_backward",
    )(grad_low, query, keys, values, up_val, *[gathered] * 6, regroup_table(), *tables)


def pro_single(scores, weight, ranks, count):
    valid = ranks < count
    head = ranks < count - 1
    peak = jnp.max(jnp.where(valid, scores, -1e30))
    expo = jnp.where(valid, jnp.exp(scores - peak), 0.0)
    later = ranks[None, :] >= ranks[:, None]
    suffix = jnp.sum(jnp.where(later, expo[None, :], 0.0), -1)
    return jnp.sum(
        jnp.where(head, -weight * (scores - peak - jnp.log(jnp.where(head, suffix, 1.0))), 0.0)
    )


def moments(first, second, grad, factor):
    clipped = grad * factor
    first_new = BETA_ONE * first + (1.0 - BETA_ONE) * clipped
    second_new = BETA_TWO * second + (1.0 - BETA_TWO) * clipped * clipped
    return (first_new, second_new)


def adam_update(weight, first, second, grad, factor):
    first_new, second_new = moments(first, second, grad, factor)
    first_hat = first_new / (1.0 - BETA_ONE**STEP)
    second_hat = second_new / (1.0 - BETA_TWO**STEP)
    weight_new = weight - LEARN_RATE * (
        first_hat / (jnp.sqrt(second_hat) + ADAM_EPS) + DECAY * weight
    )
    return (first_new, second_new, weight_new)


def body(
    token_ids,
    token_mask,
    resp_lengths,
    cand_counts,
    cand_rank,
    rewards,
    embed_table,
    embed_first,
    embed_second,
    head_table,
    head_first,
    head_second,
    qkv_weight,
    qkv_first,
    qkv_second,
    proj_weight,
    proj_first,
    proj_second,
    up_weight,
    up_first,
    up_second,
    down_weight,
    down_first,
    down_second,
    vector_params,
    vector_first,
    vector_second,
):
    slots = token_ids.shape[1]
    rows_own = slots * RESP
    core = lax.axis_index("cand")
    here = [lax.axis_index(axis) for axis in AXES]
    vocab_local = head_table.shape[0]
    pieces = split_params(vector_params)

    packed = jnp.concatenate(
        [qkv_weight, up_weight, proj_weight, *[down_weight[8 * k : 8 * k + 8] for k in range(4)]],
        axis=1,
    )
    gathered = lax.all_gather(
        packed.astype(jnp.bfloat16), ("cand", *AXES), axis=0, tiled=True
    )

    live = (
        (jnp.arange(RESP)[None, None, :] < resp_lengths[:, :, None]) & (token_mask == 1)
    ).astype(jnp.float32)
    valid = (cand_rank < cand_counts[:, None]).astype(jnp.float32)
    top_mask = (cand_rank == 0).astype(jnp.float32)
    stats = jnp.stack(
        [
            jnp.sum(valid),
            jnp.sum(rewards * valid),
            jnp.sum(rewards * rewards * valid),
            jnp.sum(live * top_mask[..., None]),
        ]
    )

    turned = jnp.concatenate(
        [token_ids[0, :, SEQ - RESP - 1 :], token_ids[0, :, : SEQ - RESP - 1]], axis=1
    )
    posted = spread(
        jnp.concatenate([turned.reshape(-1).astype(jnp.float32), stats, jnp.zeros(60)]), AXES
    )
    all_ids = posted[:, : slots * SEQ].astype(jnp.int32)
    stats = jnp.sum(posted[:, slots * SEQ : slots * SEQ + 4], 0)
    group_ids = lax.dynamic_index_in_dim(all_ids.reshape(16, RING, slots, SEQ), here[2], 1, False)
    group_targets = group_ids[:, :, 1 : RESP + 1].reshape(-1)
    flat_ids = all_ids.reshape(64, slots, 2, RESP).transpose(0, 2, 1, 3).reshape(-1)
    looked = look_up(embed_table.T, flat_ids).astype(jnp.bfloat16)
    looked = looked.reshape(16, 64, slots * SEQ).swapaxes(0, 1)
    inputs = exchange(looked, AXES).reshape(D, slots * SEQ).T.astype(jnp.float32)

    head_low = jnp.pad(head_table.astype(jnp.bfloat16), ((0, 2 * PAD_HALF - vocab_local), (0, 0)))
    head_half = lax.dynamic_slice_in_dim(head_low, core * PAD_HALF, PAD_HALF)
    head_half, inputs = lax.optimization_barrier((head_half, inputs))
    mine = spread(head_half, "z").reshape(-1, D)

    other = swap(
        jnp.concatenate([stats, rewards.reshape(-1), cand_rank.reshape(-1).astype(jnp.float32)])
    )
    stats = stats + other[:4]
    mean = stats[1] / stats[0]
    variance = stats[2] / stats[0] - mean * mean

    def both(value, second):
        return jnp.where(
            core == 0, jnp.concatenate([value, second]), jnp.concatenate([second, value])
        )

    all_rank = both(cand_rank.reshape(-1), other[4 + slots :].astype(jnp.int32))
    all_rewards = both(rewards.reshape(-1), other[4 : 4 + slots])
    weight = jax.nn.softplus((all_rewards - mean) * lax.rsqrt(variance + NORM_EPS))

    live_rows = slots * RESP
    first_rows = inputs[:live_rows]
    attn_in = layer_norm(inputs, pieces[0], pieces[1]).astype(jnp.bfloat16)
    mlp_in = layer_norm(first_rows, pieces[2], pieces[3]).astype(jnp.bfloat16)
    tables = turn_tables(slots)
    query, keys, values, mixed, up_val, act, added = layer_forward(
        attn_in, mlp_in, gathered, pieces, tables
    )
    hidden = first_rows + added + (pieces[7] + pieces[9])
    rows_low = layer_norm(hidden, pieces[4], pieces[5]).astype(jnp.bfloat16)

    rows_low, mine = lax.optimization_barrier((rows_low, mine))
    group_rows = spread(rows_low, ("x", "y")).reshape(-1, D)
    head_group = jnp.concatenate([mine, swap(mine)], axis=0)

    shard = group_targets // vocab_local
    offset = group_targets % vocab_local
    part = jnp.where(offset // PAD_HALF == core, 0, 1)
    local = (shard // RING) == here[0] * RING + here[1]
    targets = jnp.where(
        local, (part * RING + shard % RING) * PAD_HALF + offset % PAD_HALF, -1
    )
    column = jnp.arange(2 * RING * PAD_HALF)[None, :]
    half = jnp.where(column < RING * PAD_HALF, core, 1 - core)
    real = half * PAD_HALF + column % PAD_HALF < vocab_local
    logits = jnp.where(real, matmul_nt(group_rows, head_group), -1e30)
    hits = column == targets[:, None]
    local_max = jnp.max(logits, -1)
    local_sum = jnp.sum(jnp.exp(logits - local_max[:, None]), -1)
    local_target = jnp.sum(jnp.where(hits, logits, 0.0), -1)

    held = jnp.stack([local_max, local_sum, local_target], axis=1).reshape(16, rows_own, 3)
    held = exchange(held.swapaxes(1, 2), ("x", "y"))
    biggest = jnp.max(held[:, 0], 0)
    held = (
        biggest,
        jnp.sum(held[:, 1] * jnp.exp(held[:, 0] - biggest), 0),
        jnp.sum(held[:, 2], 0),
    )
    row_lse = held[0] + jnp.log(held[1])
    own_logp = (held[2] - row_lse).reshape(1, slots, RESP)
    own_count = jnp.sum(live, -1)
    own_scores = jnp.sum(own_logp * live, -1) / jnp.maximum(own_count, 1.0)
    all_scores = both(own_scores.reshape(-1), swap(own_scores.reshape(-1)))
    pro_value, pro_grad = jax.value_and_grad(pro_single)(
        all_scores, weight, all_rank, cand_counts[0]
    )
    my_grad = lax.dynamic_slice_in_dim(pro_grad, core * slots, slots).reshape(1, slots)
    sft_scale = 64 / jnp.maximum(stats[3], 1.0)
    row_grad = (
        my_grad[..., None] / jnp.maximum(own_count, 1.0)[..., None]
        - sft_scale * top_mask[..., None]
    ) * live
    back = spread(jnp.stack([row_grad.reshape(-1), row_lse]), ("x", "y"))
    group_grad = back[:, 0].reshape(-1)
    group_lse = back[:, 1].reshape(-1)

    vocab_probs = jnp.exp(logits - group_lse[:, None])
    logit_grad = (group_grad[:, None] * (hits.astype(jnp.float32) - vocab_probs)).astype(
        jnp.bfloat16
    )
    rows_part = matmul(logit_grad, head_group).astype(jnp.bfloat16)
    rows_part, logit_grad = lax.optimization_barrier((rows_part, logit_grad))
    rows_part = exchange(rows_part.reshape(16, rows_own, D), ("x", "y"))
    near = RING * PAD_HALF
    head_part = matmul_tn(logit_grad[:, :near], group_rows) + swap(
        matmul_tn(logit_grad[:, near:], group_rows).astype(jnp.bfloat16)
    ).astype(jnp.float32)
    head_part = head_part.astype(jnp.bfloat16).reshape(RING, PAD_HALF, D)
    rows_part, head_part = lax.optimization_barrier((rows_part, head_part))
    head_own = ring_sum(head_part, "z")
    rows_grad = jnp.sum(rows_part.astype(jnp.float32), 0)

    grad_hidden, gain_fin_grad, bias_fin_grad = norm_back(hidden, pieces[4], pieces[5], rows_grad)
    grad_low = grad_hidden.astype(jnp.bfloat16)
    grad_sum = jnp.sum(grad_low.astype(jnp.float32), 0)
    grad_both = of_both(grad_low)
    down_g = matmul_tn(half_of_both(act), grad_both).astype(jnp.bfloat16).reshape(64, 32, D)
    down_g = exchange(down_g, AXES)
    query_grad, key_grad, value_grad, up_grad, attn_grad, mlp_grad, *sums = layer_backward(
        grad_low, (query, keys, values, up_val), gathered, tables
    )
    attn_grad, mlp_grad, down_g = lax.optimization_barrier((attn_grad, mlp_grad, down_g))
    input_one, gain_one_grad, bias_one_grad = norm_back(inputs, pieces[0], pieces[1], attn_grad)
    input_two, gain_two_grad, bias_two_grad = norm_back(first_rows, pieces[2], pieces[3], mlp_grad)
    input_grad = input_one + jnp.pad(grad_hidden + input_two, ((0, live_rows), (0, 0)))
    attn_both = half_of_both(attn_in)
    first_both = jnp.concatenate(
        [attn_both[:live_rows], attn_both[2 * live_rows : 3 * live_rows]], axis=0
    )
    up_g = matmul_tn(half_of_both(mlp_in), of_both(up_grad)).astype(jnp.bfloat16)
    proj_g = matmul_tn(half_of_both(mixed), grad_both).astype(jnp.bfloat16)
    query_g = matmul_tn(first_both, of_both(query_grad)).astype(jnp.bfloat16)
    key_g = matmul_tn(attn_both, of_both(key_grad)).astype(jnp.bfloat16)
    value_g = matmul_tn(attn_both, of_both(value_grad)).astype(jnp.bfloat16)
    vector_head = [gain_one_grad, bias_one_grad, gain_two_grad, bias_two_grad]
    vector_tail = [*[part[0] for part in sums[:3]], grad_sum, sums[3][0], grad_sum]

    head_grad = both(head_own, swap(head_own))[:vocab_local]

    vector_grad = jnp.concatenate(vector_head + [gain_fin_grad, bias_fin_grad] + vector_tail)
    vector_high = vector_grad.astype(jnp.bfloat16)
    vector_low = (vector_grad - vector_high.astype(jnp.float32)).astype(jnp.bfloat16)
    vector_both = jnp.stack([vector_high, vector_low]).reshape(4, 64, 120).swapaxes(0, 1)
    vector_both = jnp.pad(vector_both, ((0, 0), (0, 4), (0, slots * SEQ - 120)))
    turned_grad = input_grad.astype(jnp.bfloat16).T.reshape(64, 16, slots * SEQ)
    turned_grad = jnp.concatenate([turned_grad, vector_both], axis=1)
    rest = jnp.concatenate([up_g, proj_g, query_g, key_g, value_g], axis=1).reshape(64, 8, 8 * D)
    turned_grad = exchange(turned_grad, AXES)
    embed_rows = turned_grad[:, :16].astype(jnp.float32).swapaxes(0, 1).reshape(16, -1)
    vector_both = jnp.sum(turned_grad[:, 16:20, :120].astype(jnp.float32), 0).reshape(2, 2, 120)
    vector_both = vector_both[0] + vector_both[1]
    vector_grad = lax.dynamic_index_in_dim(vector_both, core, 0, False) + swap(
        lax.dynamic_index_in_dim(vector_both, 1 - core, 0, False)
    )

    rest, embed_rows, head_own = lax.optimization_barrier((rest, embed_rows, head_own))
    rest = exchange(rest, AXES)
    embed_grad = fold(embed_rows, flat_ids, embed_table.shape[0])
    embed_grad = (embed_grad + swap(embed_grad)).T
    rest = jnp.sum(rest.astype(jnp.float32), 0)

    down_g = jnp.sum(down_g.astype(jnp.float32), 0)
    shards = (rest[:, 5 * D :], rest[:, 4 * D : 5 * D], rest[:, : 4 * D], down_g, vector_grad)
    local_squares = sum((jnp.sum(piece * piece) for piece in shards))
    local_squares = (
        local_squares + (jnp.sum(embed_grad * embed_grad) + jnp.sum(head_grad * head_grad)) / 2
    )
    sft_local = -jnp.sum(own_logp * live * top_mask[..., None])
    sums = jnp.sum(
        spread(jnp.stack([local_squares, pro_value / 2, sft_local]), ("cand", *AXES)), 0
    )
    grad_norm = jnp.sqrt(sums[0])
    factor = jnp.minimum(1.0, CLIP_NORM / (grad_norm + 1e-06))
    embed_new = adam_update(embed_table, embed_first, embed_second, embed_grad, factor)
    head_new = adam_update(head_table, head_first, head_second, head_grad, factor)
    qkv_new = adam_update(qkv_weight, qkv_first, qkv_second, shards[0], factor)
    proj_new = adam_update(proj_weight, proj_first, proj_second, shards[1], factor)
    up_new = adam_update(up_weight, up_first, up_second, shards[2], factor)
    down_new = adam_update(down_weight, down_first, down_second, shards[3], factor)
    vector_first_new, vector_second_new = moments(vector_first, vector_second, shards[4], factor)
    loss_parts = jnp.stack([sums[1], sums[2], stats[3]])
    return (
        loss_parts,
        grad_norm,
        my_grad,
        embed_new[0],
        embed_new[1],
        embed_new[2],
        head_new[0],
        head_new[1],
        head_new[2],
        qkv_new[0],
        qkv_new[1],
        qkv_new[2],
        proj_new[0],
        proj_new[1],
        proj_new[2],
        up_new[0],
        up_new[1],
        up_new[2],
        down_new[0],
        down_new[1],
        down_new[2],
        vector_first_new,
        vector_second_new,
    )


def solution(mesh):
    fine = Mesh(mesh.devices.reshape(2, RING, RING, RING), ("cand", *AXES))
    in_specs = (
        P(AXES, "cand", None),
        P(AXES, "cand", None),
        P(AXES, "cand"),
        P(AXES),
        P(AXES, "cand"),
        P(AXES, "cand"),
        P(None, AXES),
        P(None, AXES),
        P(None, AXES),
        P(AXES, None),
        P(AXES, None),
        P(AXES, None),
        P(("cand", *AXES), None),
        P(("cand", *AXES), None),
        P(("cand", *AXES), None),
        P(("cand", *AXES), None),
        P(("cand", *AXES), None),
        P(("cand", *AXES), None),
        P(("cand", *AXES), None),
        P(("cand", *AXES), None),
        P(("cand", *AXES), None),
        P(("cand", *AXES), None),
        P(("cand", *AXES), None),
        P(("cand", *AXES), None),
        P(),
        P(("cand", *AXES)),
        P(("cand", *AXES)),
    )
    out_specs = (
        P(),
        P(),
        P(AXES, "cand"),
        P(None, AXES),
        P(None, AXES),
        P(None, AXES),
        P(AXES, None),
        P(AXES, None),
        P(AXES, None),
        P(("cand", *AXES), None),
        P(("cand", *AXES), None),
        P(("cand", *AXES), None),
        P(("cand", *AXES), None),
        P(("cand", *AXES), None),
        P(("cand", *AXES), None),
        P(("cand", *AXES), None),
        P(("cand", *AXES), None),
        P(("cand", *AXES), None),
        P(("cand", *AXES), None),
        P(("cand", *AXES), None),
        P(("cand", *AXES), None),
        P(("cand", *AXES)),
        P(("cand", *AXES)),
    )
    return jax.shard_map(body, mesh=fine, in_specs=in_specs, out_specs=out_specs, check_vma=False)
```

```python
import math

import jax
import jax.numpy as jnp
import numpy as np
from jax import lax
from jax.experimental import pallas as pl
from jax.experimental.pallas import tpu as pltpu
from jax.sharding import Mesh
from jax.sharding import PartitionSpec as P

D = 1024
HEADS = 16
HEAD_DIM = 64
ROT = 16
FF = 4096
SEQ = 64
STEP = 10
RESP = 32


NORM_EPS = 1e-05
CLIP_NORM = 1.0
LEARN_RATE = 0.05
BETA_ONE = 0.9
BETA_TWO = 0.999
ADAM_EPS = 1e-08
DECAY = 0.1


RING = 4
SLOTS = 3
PAD_HALF = 448
AXES = ("x", "y", "z")


def swap(value):
    return lax.ppermute(value, "cand", [(0, 1), (1, 0)])


def exchange(pieces, axes):
    return lax.all_to_all(pieces, axes, split_axis=0, concat_axis=0, tiled=True)


def spread(value, axes):
    count = lax.axis_size(axes)
    return exchange(jnp.broadcast_to(value[None], (count, *value.shape)), axes)


def shift(value, axis, step):
    return lax.ppermute(value, axis, [(i, (i + step) % RING) for i in range(RING)])


def ring_sum(pieces, axis):
    me = lax.axis_index(axis)

    def piece(step):
        return lax.dynamic_index_in_dim(pieces, (me + step) % RING, 0, False)

    def added(first, second):
        return (first.astype(jnp.float32) + second.astype(jnp.float32)).astype(first.dtype)

    own, after, far, before = (piece(step) for step in range(RING))
    mid = far.shape[0] // 2
    back, onward = shift(far[:mid], axis, -1), shift(far[mid:], axis, 1)
    before = jnp.concatenate([added(before[:mid], back), before[mid:]], axis=0)
    after = jnp.concatenate([after[:mid], added(after[mid:], onward)], axis=0)
    got = shift(before, axis, -1).astype(jnp.float32) + shift(after, axis, 1).astype(jnp.float32)
    return own.astype(jnp.float32) + got


def of_both(value):
    return jnp.concatenate([value, swap(value)], axis=0)


def half_of_both(value):
    core = lax.axis_index("cand")
    half = value.shape[1] // 2
    kept = lax.dynamic_slice_in_dim(value, core * half, half, axis=1)
    given = lax.dynamic_slice_in_dim(value, (1 - core) * half, half, axis=1)
    return jnp.concatenate([kept, swap(given)], axis=0)


WIDE = 256
LOOK_BLOCK = 1024
FOLD_BLOCK = 2048


def look_kernel(high_ref, low_ref, table_ref, out_ref, left):
    spans = table_ref.shape[1] // WIDE
    rest = table_ref.shape[1] - spans * WIDE

    @pl.when(pl.program_id(0) == 0)
    def _():
        def fill(i, carry):
            span = table_ref[:, pl.ds(pl.multiple_of(i * WIDE, WIDE), WIDE)]
            left[pl.ds(pl.multiple_of(i * 16, 16), 16), :] = span.astype(jnp.bfloat16)
            return carry

        lax.fori_loop(0, spans, fill, 0)
        if rest:
            last = table_ref[:, spans * WIDE :].astype(jnp.bfloat16)
            left[spans * 16 :, :] = jnp.concatenate(
                [last, jnp.zeros((16, WIDE - rest), jnp.bfloat16)], axis=1
            )

    block = out_ref.shape[1]
    one_hot = jnp.where(
        lax.broadcasted_iota(jnp.int32, (WIDE, block), 0) == low_ref[...], 1.0, 0.0
    ).astype(jnp.bfloat16)
    high = jnp.broadcast_to(high_ref[...], (16, block))
    total = jnp.zeros((16, block), jnp.float32)
    rows = left.shape[0] // 16
    CH = 16
    for begin in range(0, rows, CH):
        count = min(CH, rows - begin)
        part = jnp.dot(
            left[begin * 16 : (begin + count) * 16, :], one_hot, preferred_element_type=jnp.float32
        )
        for k in range(count):
            total = total + jnp.where(high == begin + k, part[k * 16 : (k + 1) * 16], 0.0)
    out_ref[...] = total.astype(out_ref.dtype)


def look_up(table, ids):
    count = ids.shape[0]
    spans = -(-table.shape[1] // WIDE)
    high = (ids // WIDE).reshape(1, count)
    low = (ids % WIDE).reshape(1, count)
    row = pl.BlockSpec((1, LOOK_BLOCK), lambda i: (0, i))
    return pl.pallas_call(
        look_kernel,
        grid=(count // LOOK_BLOCK,),
        in_specs=[row, row, pl.BlockSpec(table.shape, lambda i: (0, 0))],
        out_specs=pl.BlockSpec((16, LOOK_BLOCK), lambda i: (0, i)),
        out_shape=jax.ShapeDtypeStruct((16, count), jnp.float32),
        scratch_shapes=[pltpu.VMEM((spans * 16, WIDE), jnp.bfloat16)],
        compiler_params=pltpu.CompilerParams(vmem_limit_bytes=40 << 20),
        cost_estimate=pl.CostEstimate(flops=2 * spans * 16 * WIDE * count, bytes_accessed=table.size * 4, transcendentals=0),
        name="look_up",
    )(high, low, table)


def fold_kernel(high_ref, low_ref, grad_ref, out_ref, left, total):
    step = pl.program_id(0)
    block = grad_ref.shape[1]
    rows = left.shape[0] // 16
    grad = grad_ref[...]
    high = jnp.broadcast_to(high_ref[...], (16, block))

    def place(i, carry):
        for k in range(4):
            at = i * 4 + k
            left[pl.ds(pl.multiple_of(at * 16, 16), 16), :] = jnp.where(
                high == at, grad, 0.0
            ).astype(jnp.bfloat16)
        return carry

    lax.fori_loop(0, rows // 4, place, 0)
    for at in range(rows // 4 * 4, rows):
        left[at * 16 : at * 16 + 16, :] = jnp.where(high == at, grad, 0.0).astype(jnp.bfloat16)
    one_hot = jnp.where(
        lax.broadcasted_iota(jnp.int32, (WIDE, block), 0) == low_ref[...], 1.0, 0.0
    ).astype(jnp.bfloat16)
    part = lax.dot_general(
        left[...], one_hot, (((1,), (1,)), ((), ())), preferred_element_type=jnp.float32
    )

    @pl.when(step == 0)
    def _():
        total[...] = part

    @pl.when(step > 0)
    def _():
        total[...] += part

    @pl.when(step == pl.num_programs(0) - 1)
    def _():
        spans = out_ref.shape[1] // WIDE
        rest = out_ref.shape[1] - spans * WIDE

        def drain(i, carry):
            out_ref[:, pl.ds(pl.multiple_of(i * WIDE, WIDE), WIDE)] = total[
                pl.ds(pl.multiple_of(i * 16, 16), 16), :
            ]
            return carry

        lax.fori_loop(0, spans, drain, 0)
        if rest:
            out_ref[:, spans * WIDE :] = total[spans * 16 :, :rest]


def fold(grads, ids, size):
    count = ids.shape[0]
    spans = -(-size // WIDE)
    high = (ids // WIDE).reshape(1, count)
    low = (ids % WIDE).reshape(1, count)
    row = pl.BlockSpec((1, FOLD_BLOCK), lambda i: (0, i))
    return pl.pallas_call(
        fold_kernel,
        grid=(count // FOLD_BLOCK,),
        in_specs=[row, row, pl.BlockSpec((16, FOLD_BLOCK), lambda i: (0, i))],
        out_specs=pl.BlockSpec((16, size), lambda i: (0, 0)),
        out_shape=jax.ShapeDtypeStruct((16, size), jnp.float32),
        scratch_shapes=[
            pltpu.VMEM((spans * 16, FOLD_BLOCK), jnp.bfloat16),
            pltpu.VMEM((spans * 16, WIDE), jnp.float32),
        ],
        compiler_params=pltpu.CompilerParams(vmem_limit_bytes=40 << 20),
        cost_estimate=pl.CostEstimate(flops=2 * spans * 16 * WIDE * count, bytes_accessed=size * 64, transcendentals=0),
        name="fold",
    )(high, low, grads)


def matmul(left, right):
    return jnp.dot(left, right, preferred_element_type=jnp.float32)


def matmul_tn(left, right):
    return lax.dot_general(
        left, right, (((0,), (0,)), ((), ())), preferred_element_type=jnp.float32
    )


def matmul_nt(left, right):
    return lax.dot_general(
        left, right, (((1,), (1,)), ((), ())), preferred_element_type=jnp.float32
    )


def layer_norm(inputs, gain, bias):
    mean = jnp.mean(inputs, -1, keepdims=True)
    centred = inputs - mean
    variance = jnp.mean(centred * centred, -1, keepdims=True)
    return centred * lax.rsqrt(variance + NORM_EPS) * gain + bias


def norm_back(inputs, gain, bias, grad):
    outputs, pullback = jax.vjp(layer_norm, inputs, gain, bias)
    return pullback(grad)


def split_params(vector):
    spans = [D, D, D, D, D, D, 3 * D, D, FF, D]
    pieces = []
    begin = 0
    for span_len in spans:
        pieces.append(vector[begin : begin + span_len])
        begin = begin + span_len
    return pieces


def turn(values, tables, sign):
    cosine, low, high = tables
    return (
        values * cosine
        + sign * (pltpu.roll(values, 120, axis=1) * low + pltpu.roll(values, 8, axis=1) * high)
    )


def dot_nn(left, right):
    return jnp.dot(left, right, preferred_element_type=jnp.float32)


def dot_nt(left, right):
    return lax.dot_general(
        left, right, (((1,), (1,)), ((), ())), preferred_element_type=jnp.float32
    )


def dot_tn(left, right):
    return lax.dot_general(
        left, right, (((0,), (0,)), ((), ())), preferred_element_type=jnp.float32
    )


def pair_of(values):
    lanes = lax.broadcasted_iota(jnp.int32, values.shape, 1)
    zero = jnp.zeros_like(values)
    return (jnp.where(lanes < HEAD_DIM, values, zero), jnp.where(lanes < HEAD_DIM, zero, values))


def row_places(rows, width, axis):
    row = lax.broadcasted_iota(jnp.int32, (rows, width), axis)
    live = SLOTS * RESP
    late = row >= live
    row = jnp.where(late, row - live, row)
    inside = row % RESP
    place = jnp.where(
        late, jnp.where(inside == 0, SEQ - 1, inside - 1), inside + (SEQ - RESP - 1)
    )
    return row // RESP, place


def softmax_rows(query, keys):
    rows, width = query.shape[0], keys.shape[0]
    scores = dot_nt(query, keys) * HEAD_DIM ** (-0.5)
    query_slot, query_place = row_places(rows, width, 0)
    key_slot, key_place = row_places(rows, width, 1)
    seen = (query_slot == key_slot) & (query_place >= key_place)
    scores = jnp.where(seen, scores, -1e30)
    scores = jnp.exp(scores - jnp.max(scores, axis=1, keepdims=True))
    return scores / jnp.sum(scores, axis=1, keepdims=True)


def forward_kernel(
    attn_ref, mlp_ref, query_w, key_w, value_w, proj_w, up_w, down_w,
    query_b, key_b, value_b, up_b, regroup, cosine, low, high,
    query_ref, key_ref, value_ref, mixed_ref, up_ref, act_ref, out_ref,
):
    live = query_ref.shape[0]
    tables = (cosine[...], low[...], high[...])
    firsts = tuple(table[:live] for table in tables)
    attn = attn_ref[...]
    query = turn(dot_nn(attn[:live], query_w[...]) + query_b[...], firsts, 1.0).astype(jnp.bfloat16)
    keys = turn(dot_nn(attn, key_w[...]) + key_b[...], tables, 1.0).astype(jnp.bfloat16)
    values = (dot_nn(attn, value_w[...]) + value_b[...]).astype(jnp.bfloat16)
    query_ref[...] = query
    key_ref[...] = keys
    value_ref[...] = values
    mixed = 0.0
    for part, held in zip(pair_of(query), pair_of(values)):
        probs = softmax_rows(part, keys).astype(jnp.bfloat16)
        mixed = mixed + dot_nn(probs, held)
    mixed = mixed.astype(jnp.bfloat16)
    mixed_ref[...] = mixed
    up_val = dot_nn(mlp_ref[...], up_w[...]) + up_b[...]
    act = (0.5 * up_val * (1.0 + lax.erf(up_val * 0.5**0.5))).astype(jnp.bfloat16)
    up_ref[...] = up_val
    act_ref[...] = act
    part = dot_nn(mixed, proj_w[...])
    act = dot_nn(act, regroup[...]).astype(jnp.bfloat16)
    for k in range(4):
        part = part + dot_nn(act[:, 128 * k : 128 * k + 128], down_w[:, D * k : D * k + D])

    @pl.when(pl.program_id(0) == 0)
    def _():
        out_ref[...] = part

    @pl.when(pl.program_id(0) > 0)
    def _():
        out_ref[...] += part


def backward_kernel(
    grad_ref, query_ref, key_ref, value_ref, up_ref, query_w, key_w, value_w, proj_w, up_w, down_w,
    regroup, cosine, low, high,
    query_g, key_g, value_g, up_g, attn_g, mlp_g, query_s, key_s, value_s, up_s,
):
    live = query_ref.shape[0]
    tables = (cosine[...], low[...], high[...])
    firsts = tuple(table[:live] for table in tables)
    grad = grad_ref[...]
    query, keys, values = query_ref[...], key_ref[...], value_ref[...]
    mixed_grad = dot_nt(grad, proj_w[...]).astype(jnp.bfloat16)
    query_grad, key_grad, value_grad = 0.0, 0.0, 0.0
    for part, held, given in zip(pair_of(query), pair_of(keys), pair_of(mixed_grad)):
        probs = softmax_rows(part, keys)
        probs_grad = dot_nt(given, values)
        value_grad = value_grad + dot_tn(probs.astype(jnp.bfloat16), given)
        score_grad = probs * (probs_grad - jnp.sum(probs * probs_grad, axis=1, keepdims=True))
        score_grad = score_grad.astype(jnp.bfloat16)
        query_grad = query_grad + dot_nn(score_grad, held)
        key_grad = key_grad + dot_tn(score_grad, part)
    scale = HEAD_DIM ** (-0.5)
    query_grad = turn(query_grad * scale, firsts, -1.0).astype(jnp.bfloat16)
    key_grad = turn(key_grad * scale, tables, -1.0).astype(jnp.bfloat16)
    value_grad = value_grad.astype(jnp.bfloat16)
    act_grad = jnp.concatenate(
        [dot_nt(grad, down_w[:, D * k : D * k + D]) for k in range(4)], axis=1
    )
    act_high = act_grad.astype(jnp.bfloat16)
    act_low = (act_grad - act_high.astype(jnp.float32)).astype(jnp.bfloat16)
    act_grad = dot_nt(act_high, regroup[...]) + dot_nt(act_low, regroup[...])
    up_val = up_ref[...]
    slope = 0.5 * (1.0 + lax.erf(up_val * 0.5**0.5)) + up_val * (
        jnp.exp(-0.5 * up_val * up_val) * (2.0 * math.pi) ** (-0.5)
    )
    up_grad = (act_grad * slope).astype(jnp.bfloat16)
    for ref, sums, value in (
        (query_g, query_s, query_grad),
        (key_g, key_s, key_grad),
        (value_g, value_s, value_grad),
        (up_g, up_s, up_grad),
    ):
        ref[...] = value
        sums[...] = jnp.sum(value.astype(jnp.float32), axis=0, keepdims=True)
    first = dot_nt(query_grad, query_w[...])
    both = dot_nt(key_grad, key_w[...]) + dot_nt(value_grad, value_w[...])
    mlp = dot_nt(up_grad, up_w[...])

    @pl.when(pl.program_id(0) == 0)
    def _():
        attn_g[...] = both
        attn_g[:live] += first
        mlp_g[...] = mlp

    @pl.when(pl.program_id(0) > 0)
    def _():
        attn_g[...] += both
        attn_g[:live] += first
        mlp_g[...] += mlp


def turn_tables(slots):
    half = ROT // 2
    row = np.arange(2 * slots * RESP)
    inside = row % RESP
    place = np.where(row < slots * RESP, inside + SEQ - RESP - 1, (inside - 1) % SEQ)
    lane = np.arange(2 * HEAD_DIM) % HEAD_DIM
    freq = np.float32(10000.0) ** (-(np.arange(half) * np.float32(2.0 / ROT)).astype(np.float32))
    angle = place.astype(np.float32)[:, None] * freq.astype(np.float32)[lane % half][None, :]
    cosine = np.where(lane < ROT, np.cos(angle), 1.0).astype(np.float32)
    sine = np.sin(angle)
    low = np.where(lane < half, -sine, 0.0).astype(np.float32)
    high = np.where((lane >= half) & (lane < ROT), sine, 0.0).astype(np.float32)
    return cosine, low, high


def regroup_table():
    at = np.arange(512)
    to = (at // 8 % 4) * 128 + (at // 32) * 8 + at % 8
    table = np.zeros((512, 512), np.float32)
    table[at, to] = 1.0
    return jnp.asarray(table, jnp.bfloat16)


def weight_specs():
    wide = 2 * HEAD_DIM
    return [
        pl.BlockSpec((D, wide), lambda j: (0, j)),
        pl.BlockSpec((D, wide), lambda j: (0, 8 + j)),
        pl.BlockSpec((D, wide), lambda j: (0, 16 + j)),
        pl.BlockSpec((wide, D), lambda j: (j, 7)),
        pl.BlockSpec((D, 512), lambda j: (0, 6 + j)),
        pl.BlockSpec((128, 4 * D), lambda j: (j, 2)),
    ]


def whole(*shape):
    return pl.BlockSpec(shape, lambda j: (0, 0))


def columns(rows, width):
    return pl.BlockSpec((rows, width), lambda j: (0, j))


def layer_forward(attn_in, mlp_in, gathered, pieces, tables):
    rows, live = attn_in.shape[0], mlp_in.shape[0]
    wide = 2 * HEAD_DIM
    bias = pieces[6].reshape(1, 3 * D)
    shape = jax.ShapeDtypeStruct
    return pl.pallas_call(
        forward_kernel,
        grid=(HEADS // 2,),
        in_specs=[whole(rows, D), whole(live, D)]
        + weight_specs()
        + [
            pl.BlockSpec((1, wide), lambda j: (0, j)),
            pl.BlockSpec((1, wide), lambda j: (0, 8 + j)),
            pl.BlockSpec((1, wide), lambda j: (0, 16 + j)),
            columns(1, 512),
        ]
        + [whole(512, 512)]
        + [whole(rows, wide)] * 3,
        out_specs=[
            columns(live, wide),
            columns(rows, wide),
            columns(rows, wide),
            columns(live, wide),
            columns(live, 512),
            columns(live, 512),
            whole(live, D),
        ],
        out_shape=[
            shape((live, D), jnp.bfloat16),
            shape((rows, D), jnp.bfloat16),
            shape((rows, D), jnp.bfloat16),
            shape((live, D), jnp.bfloat16),
            shape((live, FF), jnp.float32),
            shape((live, FF), jnp.bfloat16),
            shape((live, D), jnp.float32),
        ],
        compiler_params=pltpu.CompilerParams(vmem_limit_bytes=40 << 20),
        cost_estimate=pl.CostEstimate(
            flops=2 * live * 16 * D * D, bytes_accessed=64 * D * D, transcendentals=0
        ),
        name="layer_forward",
    )(attn_in, mlp_in, *[gathered] * 6, bias, bias, bias, pieces[8].reshape(1, FF), regroup_table(), *tables)


def layer_backward(grad_low, saved, gathered, tables):
    query, keys, values, up_val = saved
    rows, live = keys.shape[0], query.shape[0]
    wide = 2 * HEAD_DIM
    shape = jax.ShapeDtypeStruct
    return pl.pallas_call(
        backward_kernel,
        grid=(HEADS // 2,),
        in_specs=[
            whole(live, D),
            columns(live, wide),
            columns(rows, wide),
            columns(rows, wide),
            columns(live, 512),
        ]
        + weight_specs()
        + [whole(512, 512)]
        + [whole(rows, wide)] * 3,
        out_specs=[
            columns(live, wide),
            columns(rows, wide),
            columns(rows, wide),
            columns(live, 512),
            whole(rows, D),
            whole(live, D),
            columns(1, wide),
            columns(1, wide),
            columns(1, wide),
            columns(1, 512),
        ],
        out_shape=[
            shape((live, D), jnp.bfloat16),
            shape((rows, D), jnp.bfloat16),
            shape((rows, D), jnp.bfloat16),
            shape((live, FF), jnp.bfloat16),
            shape((rows, D), jnp.float32),
            shape((live, D), jnp.float32),
            shape((1, D), jnp.float32),
            shape((1, D), jnp.float32),
            shape((1, D), jnp.float32),
            shape((1, FF), jnp.float32),
        ],
        compiler_params=pltpu.CompilerParams(vmem_limit_bytes=40 << 20),
        cost_estimate=pl.CostEstimate(
            flops=2 * live * 16 * D * D, bytes_accessed=64 * D * D, transcendentals=0
        ),
        name="layer_backward",
    )(grad_low, query, keys, values, up_val, *[gathered] * 6, regroup_table(), *tables)


def pro_single(scores, weight, ranks, count):
    valid = ranks < count
    head = ranks < count - 1
    peak = jnp.max(jnp.where(valid, scores, -1e30))
    expo = jnp.where(valid, jnp.exp(scores - peak), 0.0)
    later = ranks[None, :] >= ranks[:, None]
    suffix = jnp.sum(jnp.where(later, expo[None, :], 0.0), -1)
    return jnp.sum(
        jnp.where(head, -weight * (scores - peak - jnp.log(jnp.where(head, suffix, 1.0))), 0.0)
    )


def moments(first, second, grad, factor):
    clipped = grad * factor
    first_new = BETA_ONE * first + (1.0 - BETA_ONE) * clipped
    second_new = BETA_TWO * second + (1.0 - BETA_TWO) * clipped * clipped
    return (first_new, second_new)


def adam_update(weight, first, second, grad, factor):
    first_new, second_new = moments(first, second, grad, factor)
    first_hat = first_new / (1.0 - BETA_ONE**STEP)
    second_hat = second_new / (1.0 - BETA_TWO**STEP)
    weight_new = weight - LEARN_RATE * (
        first_hat / (jnp.sqrt(second_hat) + ADAM_EPS) + DECAY * weight
    )
    return (first_new, second_new, weight_new)


def body(
    token_ids,
    token_mask,
    resp_lengths,
    cand_counts,
    cand_rank,
    rewards,
    embed_table,
    embed_first,
    embed_second,
    head_table,
    head_first,
    head_second,
    qkv_weight,
    qkv_first,
    qkv_second,
    proj_weight,
    proj_first,
    proj_second,
    up_weight,
    up_first,
    up_second,
    down_weight,
    down_first,
    down_second,
    vector_params,
    vector_first,
    vector_second,
):
    slots = token_ids.shape[1]
    rows_own = slots * RESP
    core = lax.axis_index("cand")
    here = [lax.axis_index(axis) for axis in AXES]
    vocab_local = head_table.shape[0]
    pieces = split_params(vector_params)

    packed = jnp.concatenate(
        [qkv_weight, up_weight, proj_weight, *[down_weight[8 * k : 8 * k + 8] for k in range(4)]],
        axis=1,
    )
    gathered = lax.all_gather(
        packed.astype(jnp.bfloat16), ("cand", *AXES), axis=0, tiled=True
    )

    live = (
        (jnp.arange(RESP)[None, None, :] < resp_lengths[:, :, None]) & (token_mask == 1)
    ).astype(jnp.float32)
    valid = (cand_rank < cand_counts[:, None]).astype(jnp.float32)
    top_mask = (cand_rank == 0).astype(jnp.float32)
    stats = jnp.stack(
        [
            jnp.sum(valid),
            jnp.sum(rewards * valid),
            jnp.sum(rewards * rewards * valid),
            jnp.sum(live * top_mask[..., None]),
        ]
    )

    turned = jnp.concatenate(
        [token_ids[0, :, SEQ - RESP - 1 :], token_ids[0, :, : SEQ - RESP - 1]], axis=1
    )
    posted = spread(
        jnp.concatenate([turned.reshape(-1).astype(jnp.float32), stats, jnp.zeros(60)]), AXES
    )
    all_ids = posted[:, : slots * SEQ].astype(jnp.int32)
    stats = jnp.sum(posted[:, slots * SEQ : slots * SEQ + 4], 0)
    group_ids = lax.dynamic_index_in_dim(all_ids.reshape(16, RING, slots, SEQ), here[2], 1, False)
    group_targets = group_ids[:, :, 1 : RESP + 1].reshape(-1)
    flat_ids = all_ids.reshape(64, slots, 2, RESP).transpose(0, 2, 1, 3).reshape(-1)
    looked = look_up(embed_table.T, flat_ids).astype(jnp.bfloat16)
    looked = looked.reshape(16, 64, slots * SEQ).swapaxes(0, 1)
    inputs = exchange(looked, AXES).reshape(D, slots * SEQ).T.astype(jnp.float32)

    head_low = jnp.pad(head_table.astype(jnp.bfloat16), ((0, 2 * PAD_HALF - vocab_local), (0, 0)))
    head_half = lax.dynamic_slice_in_dim(head_low, core * PAD_HALF, PAD_HALF)
    head_half, inputs = lax.optimization_barrier((head_half, inputs))
    mine = spread(head_half, "z").reshape(-1, D)

    other = swap(
        jnp.concatenate([stats, rewards.reshape(-1), cand_rank.reshape(-1).astype(jnp.float32)])
    )
    stats = stats + other[:4]
    mean = stats[1] / stats[0]
    variance = stats[2] / stats[0] - mean * mean

    def both(value, second):
        return jnp.where(
            core == 0, jnp.concatenate([value, second]), jnp.concatenate([second, value])
        )

    all_rank = both(cand_rank.reshape(-1), other[4 + slots :].astype(jnp.int32))
    all_rewards = both(rewards.reshape(-1), other[4 : 4 + slots])
    weight = jax.nn.softplus((all_rewards - mean) * lax.rsqrt(variance + NORM_EPS))

    live_rows = slots * RESP
    first_rows = inputs[:live_rows]
    attn_in = layer_norm(inputs, pieces[0], pieces[1]).astype(jnp.bfloat16)
    mlp_in = layer_norm(first_rows, pieces[2], pieces[3]).astype(jnp.bfloat16)
    tables = turn_tables(slots)
    query, keys, values, mixed, up_val, act, added = layer_forward(
        attn_in, mlp_in, gathered, pieces, tables
    )
    hidden = first_rows + added + (pieces[7] + pieces[9])
    rows_low = layer_norm(hidden, pieces[4], pieces[5]).astype(jnp.bfloat16)

    rows_low, mine = lax.optimization_barrier((rows_low, mine))
    group_rows = spread(rows_low, ("x", "y")).reshape(-1, D)
    head_group = jnp.concatenate([mine, swap(mine)], axis=0)

    shard = group_targets // vocab_local
    offset = group_targets % vocab_local
    part = jnp.where(offset // PAD_HALF == core, 0, 1)
    local = (shard // RING) == here[0] * RING + here[1]
    targets = jnp.where(
        local, (part * RING + shard % RING) * PAD_HALF + offset % PAD_HALF, -1
    )
    column = jnp.arange(2 * RING * PAD_HALF)[None, :]
    half = jnp.where(column < RING * PAD_HALF, core, 1 - core)
    real = half * PAD_HALF + column % PAD_HALF < vocab_local
    logits = jnp.where(real, matmul_nt(group_rows, head_group), -1e30)
    hits = column == targets[:, None]
    local_max = jnp.max(logits, -1)
    local_sum = jnp.sum(jnp.exp(logits - local_max[:, None]), -1)
    local_target = jnp.sum(jnp.where(hits, logits, 0.0), -1)

    held = jnp.stack([local_max, local_sum, local_target], axis=1).reshape(16, rows_own, 3)
    held = exchange(held.swapaxes(1, 2), ("x", "y"))
    biggest = jnp.max(held[:, 0], 0)
    held = (
        biggest,
        jnp.sum(held[:, 1] * jnp.exp(held[:, 0] - biggest), 0),
        jnp.sum(held[:, 2], 0),
    )
    row_lse = held[0] + jnp.log(held[1])
    own_logp = (held[2] - row_lse).reshape(1, slots, RESP)
    own_count = jnp.sum(live, -1)
    own_scores = jnp.sum(own_logp * live, -1) / jnp.maximum(own_count, 1.0)
    all_scores = both(own_scores.reshape(-1), swap(own_scores.reshape(-1)))
    pro_value, pro_grad = jax.value_and_grad(pro_single)(
        all_scores, weight, all_rank, cand_counts[0]
    )
    my_grad = lax.dynamic_slice_in_dim(pro_grad, core * slots, slots).reshape(1, slots)
    sft_scale = 64 / jnp.maximum(stats[3], 1.0)
    row_grad = (
        my_grad[..., None] / jnp.maximum(own_count, 1.0)[..., None]
        - sft_scale * top_mask[..., None]
    ) * live
    back = spread(jnp.stack([row_grad.reshape(-1), row_lse]), ("x", "y"))
    group_grad = back[:, 0].reshape(-1)
    group_lse = back[:, 1].reshape(-1)

    vocab_probs = jnp.exp(logits - group_lse[:, None])
    logit_grad = (group_grad[:, None] * (hits.astype(jnp.float32) - vocab_probs)).astype(
        jnp.bfloat16
    )
    rows_part = matmul(logit_grad, head_group).astype(jnp.bfloat16)
    rows_part, logit_grad = lax.optimization_barrier((rows_part, logit_grad))
    rows_part = exchange(rows_part.reshape(16, rows_own, D), ("x", "y"))
    near = RING * PAD_HALF
    head_part = matmul_tn(logit_grad[:, :near], group_rows) + swap(
        matmul_tn(logit_grad[:, near:], group_rows).astype(jnp.bfloat16)
    ).astype(jnp.float32)
    head_part = head_part.astype(jnp.bfloat16).reshape(RING, PAD_HALF, D)
    rows_part, head_part = lax.optimization_barrier((rows_part, head_part))
    head_own = ring_sum(head_part, "z")
    rows_grad = jnp.sum(rows_part.astype(jnp.float32), 0)

    grad_hidden, gain_fin_grad, bias_fin_grad = norm_back(hidden, pieces[4], pieces[5], rows_grad)
    grad_low = grad_hidden.astype(jnp.bfloat16)
    grad_sum = jnp.sum(grad_low.astype(jnp.float32), 0)
    grad_both = of_both(grad_low)
    down_g = matmul_tn(half_of_both(act), grad_both).astype(jnp.bfloat16).reshape(64, 32, D)
    proj_g = matmul_tn(half_of_both(mixed), grad_both).astype(jnp.bfloat16).reshape(64, 8, D)
    early = exchange(jnp.concatenate([down_g, proj_g], axis=1), AXES)
    query_grad, key_grad, value_grad, up_grad, attn_grad, mlp_grad, *sums = layer_backward(
        grad_low, (query, keys, values, up_val), gathered, tables
    )
    attn_grad, mlp_grad, early = lax.optimization_barrier((attn_grad, mlp_grad, early))
    input_one, gain_one_grad, bias_one_grad = norm_back(inputs, pieces[0], pieces[1], attn_grad)
    input_two, gain_two_grad, bias_two_grad = norm_back(first_rows, pieces[2], pieces[3], mlp_grad)
    input_grad = input_one + jnp.pad(grad_hidden + input_two, ((0, live_rows), (0, 0)))
    attn_both = half_of_both(attn_in)
    first_both = jnp.concatenate(
        [attn_both[:live_rows], attn_both[2 * live_rows : 3 * live_rows]], axis=0
    )
    up_g = matmul_tn(half_of_both(mlp_in), of_both(up_grad)).astype(jnp.bfloat16)
    query_g = matmul_tn(first_both, of_both(query_grad)).astype(jnp.bfloat16)
    key_g = matmul_tn(attn_both, of_both(key_grad)).astype(jnp.bfloat16)
    value_g = matmul_tn(attn_both, of_both(value_grad)).astype(jnp.bfloat16)
    vector_head = [gain_one_grad, bias_one_grad, gain_two_grad, bias_two_grad]
    vector_tail = [*[part[0] for part in sums[:3]], grad_sum, sums[3][0], grad_sum]

    head_grad = both(head_own, swap(head_own))[:vocab_local]

    vector_grad = jnp.concatenate(vector_head + [gain_fin_grad, bias_fin_grad] + vector_tail)
    vector_high = vector_grad.astype(jnp.bfloat16)
    vector_low = (vector_grad - vector_high.astype(jnp.float32)).astype(jnp.bfloat16)
    vector_both = jnp.stack([vector_high, vector_low]).reshape(4, 64, 120).swapaxes(0, 1)
    vector_both = jnp.pad(vector_both, ((0, 0), (0, 4), (0, slots * SEQ - 120)))
    turned_grad = input_grad.astype(jnp.bfloat16).T.reshape(64, 16, slots * SEQ)
    turned_grad = jnp.concatenate([turned_grad, vector_both], axis=1)
    rest = jnp.concatenate([up_g, query_g, key_g, value_g], axis=1).reshape(64, 8, 7 * D)
    turned_grad = exchange(turned_grad, AXES)
    embed_rows = turned_grad[:, :16].astype(jnp.float32).swapaxes(0, 1).reshape(16, -1)
    vector_both = jnp.sum(turned_grad[:, 16:20, :120].astype(jnp.float32), 0).reshape(2, 2, 120)
    vector_both = vector_both[0] + vector_both[1]
    vector_grad = lax.dynamic_index_in_dim(vector_both, core, 0, False) + swap(
        lax.dynamic_index_in_dim(vector_both, 1 - core, 0, False)
    )

    rest, embed_rows, head_own = lax.optimization_barrier((rest, embed_rows, head_own))
    rest = exchange(rest, AXES)
    embed_grad = fold(embed_rows, flat_ids, embed_table.shape[0])
    embed_grad = (embed_grad + swap(embed_grad)).T
    rest = jnp.sum(rest.astype(jnp.float32), 0)

    early = jnp.sum(early.astype(jnp.float32), 0)
    shards = (rest[:, 4 * D :], early[32:], rest[:, : 4 * D], early[:32], vector_grad)
    local_squares = sum((jnp.sum(piece * piece) for piece in shards))
    local_squares = (
        local_squares + (jnp.sum(embed_grad * embed_grad) + jnp.sum(head_grad * head_grad)) / 2
    )
    sft_local = -jnp.sum(own_logp * live * top_mask[..., None])
    sums = jnp.sum(
        spread(jnp.stack([local_squares, pro_value / 2, sft_local]), ("cand", *AXES)), 0
    )
    grad_norm = jnp.sqrt(sums[0])
    factor = jnp.minimum(1.0, CLIP_NORM / (grad_norm + 1e-06))
    embed_new = adam_update(embed_table, embed_first, embed_second, embed_grad, factor)
    head_new = adam_update(head_table, head_first, head_second, head_grad, factor)
    qkv_new = adam_update(qkv_weight, qkv_first, qkv_second, shards[0], factor)
    proj_new = adam_update(proj_weight, proj_first, proj_second, shards[1], factor)
    up_new = adam_update(up_weight, up_first, up_second, shards[2], factor)
    down_new = adam_update(down_weight, down_first, down_second, shards[3], factor)
    vector_first_new, vector_second_new = moments(vector_first, vector_second, shards[4], factor)
    loss_parts = jnp.stack([sums[1], sums[2], stats[3]])
    return (
        loss_parts,
        grad_norm,
        my_grad,
        embed_new[0],
        embed_new[1],
        embed_new[2],
        head_new[0],
        head_new[1],
        head_new[2],
        qkv_new[0],
        qkv_new[1],
        qkv_new[2],
        proj_new[0],
        proj_new[1],
        proj_new[2],
        up_new[0],
        up_new[1],
        up_new[2],
        down_new[0],
        down_new[1],
        down_new[2],
        vector_first_new,
        vector_second_new,
    )


def solution(mesh):
    fine = Mesh(mesh.devices.reshape(2, RING, RING, RING), ("cand", *AXES))
    in_specs = (
        P(AXES, "cand", None),
        P(AXES, "cand", None),
        P(AXES, "cand"),
        P(AXES),
        P(AXES, "cand"),
        P(AXES, "cand"),
        P(None, AXES),
        P(None, AXES),
        P(None, AXES),
        P(AXES, None),
        P(AXES, None),
        P(AXES, None),
        P(("cand", *AXES), None),
        P(("cand", *AXES), None),
        P(("cand", *AXES), None),
        P(("cand", *AXES), None),
        P(("cand", *AXES), None),
        P(("cand", *AXES), None),
        P(("cand", *AXES), None),
        P(("cand", *AXES), None),
        P(("cand", *AXES), None),
        P(("cand", *AXES), None),
        P(("cand", *AXES), None),
        P(("cand", *AXES), None),
        P(),
        P(("cand", *AXES)),
        P(("cand", *AXES)),
    )
    out_specs = (
        P(),
        P(),
        P(AXES, "cand"),
        P(None, AXES),
        P(None, AXES),
        P(None, AXES),
        P(AXES, None),
        P(AXES, None),
        P(AXES, None),
        P(("cand", *AXES), None),
        P(("cand", *AXES), None),
        P(("cand", *AXES), None),
        P(("cand", *AXES), None),
        P(("cand", *AXES), None),
        P(("cand", *AXES), None),
        P(("cand", *AXES), None),
        P(("cand", *AXES), None),
        P(("cand", *AXES), None),
        P(("cand", *AXES), None),
        P(("cand", *AXES), None),
        P(("cand", *AXES), None),
        P(("cand", *AXES)),
        P(("cand", *AXES)),
    )
    return jax.shard_map(body, mesh=fine, in_specs=in_specs, out_specs=out_specs, check_vma=False)
```
